512 devices in a mesh: tm: 64 (over x, z_hi, y), head: 8 (over z_lo, core).
Axes of the slice: x: 4, y: 8, z: 8 (z_hi: 2, z_lo: 4; z = z_hi * 4 + z_lo), core: 2. Of those that a mesh axis runs over, the one named last changes fastest.
Arguments:
- queries: bfloat16 [8192, 3072], P('tm', 'head'), may hold values from -22 to 22
- keys: bfloat16 [8192, 3072], P('tm', 'head'), may hold values from -4 to 4
- values: bfloat16 [8192, 3072], P('tm', 'head'), may hold values from -5 to 5
- latents: bfloat16 [8192, 64], P('tm'), may hold values from -3 to 3
- out_weight: bfloat16 [3072, 64], P('head'), may hold values from -0.21875 to 0.21875
- step_size: float32 [64], replicated, may hold values from 0.5 to 2
- conv_weight: bfloat16 [3, 64, 512], P(None, None, 'head'), may hold values from -0.4375 to 0.4375
- span_of_slot: int32 [64], replicated, may hold values from 0 to 63, each once
- valid_count: int32 [64], replicated, may hold values from 32 to 128, as said below
- decoder_order: int32 [128], replicated, may hold values from 0 to 127, each once
Outputs:
- denoised: bfloat16 [128, 64, 64], P('tm')
- features: bfloat16 [128, 64, 512], P('tm', None, 'head')
The draws below stay inside these ranges and needn't reach their ends.
Inputs may be any that keep to these rules, and one draw needn't show every extreme that they name: `valid_count`: at least one span is full and one holds 32 live tokens.
All inputs are finite; a program needn't handle non-finite values.
Results may differ from the reference program's by a relative error of at most 0.017.
Values may be sent and summed in bfloat16 or wider, within the bound.
A program may use at most 64 MiB of HBM per device.

```python
import math
import jax
import jax.numpy as jnp
from jax import lax

HD = 128
HPD = 3
LAT = 64
COUT = 512
KT = 3
TOK_DEV = 128
HEADS = 24
NCHUNK = 64
TOKENS = 8192
N_TM = 64
N_HEAD = 8


def draw_keys(key, part):
    key = jax.random.fold_in(key, 11)
    width = HPD * N_HEAD * HD
    base = jnp.clip(jax.random.normal(key, (TOKENS, width), jnp.float32), -4.0, 4.0)
    return base.astype(jnp.bfloat16)


def draw_queries(key, part):
    key = jax.random.fold_in(key, 12)
    width = HPD * N_HEAD * HD
    base = jnp.clip(2.5 * jax.random.normal(key, (TOKENS, width), jnp.float32), -10.0, 10.0)
    return base.astype(jnp.bfloat16)


def draw_valid_count(key, part):
    key = jax.random.fold_in(key, 21)
    first, second = jax.random.split(key)
    counts = jax.random.randint(first, (N_TM,), TOK_DEV // 4, TOK_DEV + 1)
    full_span = jax.random.randint(second, (), 0, N_TM)
    counts = counts.at[full_span].set(TOK_DEV)
    counts = counts.at[(full_span + 1) % N_TM].set(TOK_DEV // 4)
    return counts.astype(jnp.int32)


def block_scale(own_key, extent, shards, least, top_value):
    gain, own = 1.0, jax.random.fold_in(own_key, 6)
    for position, blocks in shards:
        heights = jnp.exp(jax.random.uniform(jax.random.fold_in(own, position), (blocks,), jnp.float32, least / len(shards), top_value / len(shards)))
        gain = gain * jnp.repeat(heights, extent[position] // blocks).reshape([-1 if axis == position else 1 for axis in range(len(extent))])
    return gain


def bell_draw(own_key, extent, deviation, reach, cuts=(), kind=jnp.bfloat16):
    gain = block_scale(own_key, extent, cuts, -0.22, 0.18) if cuts else 1.0
    values = jax.random.normal(own_key, extent, jnp.float32) * deviation * gain
    return jnp.minimum(jnp.maximum(values, -reach), reach).astype(kind)


def setup_inputs(seed: int = 0) -> dict:
    splits = jax.random.split(jax.random.key(seed), 11)
    return {
        "queries": draw_queries(jax.random.fold_in(splits[10], 71), 0),
        "keys": draw_keys(jax.random.fold_in(splits[10], 71), 0),
        "values": bell_draw(splits[2], (TOKENS, HEADS * HD), 1.0, 5.0, ((0, 64), (1, 8))),
        "latents": bell_draw(splits[3], (TOKENS, LAT), 0.5, 3.0, ((0, 64),)),
        "out_weight": bell_draw(splits[4], (HEADS * HD, LAT), (HEADS * HD // 4) ** -0.5, 0.21875, ((0, 8),)),
        "step_size": jnp.clip(jnp.exp(jax.random.uniform(splits[5], (NCHUNK,), jnp.float32, math.log(0.5), math.log(2.0))), 0.5, 2.0),
        "conv_weight": bell_draw(splits[6], (KT, LAT, COUT), (KT * LAT) ** -0.5, 0.4375, ((2, 8),)),
        "span_of_slot": jax.random.permutation(splits[7], NCHUNK).astype(jnp.int32),
        "valid_count": draw_valid_count(jax.random.fold_in(splits[10], 71), 0),
        "decoder_order": jax.random.permutation(splits[9], TOK_DEV).astype(jnp.int32),
    }


def reference(queries, keys, values, latents, out_weight, step_size, conv_weight, span_of_slot, valid_count, decoder_order):
    rows = jnp.arange(TOKENS, dtype=jnp.int32)
    row_span = span_of_slot[rows // TOK_DEV]
    row_live = (rows % TOK_DEV) < valid_count[row_span]
    heads_all = HPD * N_HEAD
    key_full = keys.astype(jnp.float32).reshape(TOKENS, heads_all, HD)
    value_full = values.astype(jnp.float32).reshape(TOKENS, heads_all, HD)
    score_scale = 1.0 / (HD ** 0.5)

    def one_slot(slot):
        start = (slot * TOK_DEV).astype(jnp.int32)
        query_rows = lax.dynamic_slice_in_dim(queries, start, TOK_DEV, 0)
        query_rows = query_rows.astype(jnp.float32).reshape(TOK_DEV, heads_all, HD)
        own_span = span_of_slot[slot]
        allowed = row_live & (row_span <= own_span)
        scores = jnp.einsum("qhd,khd->hqk", query_rows, key_full) * score_scale
        scores = jnp.where(allowed[None, None, :], scores, -jnp.inf)
        row_max = jnp.max(scores, axis=-1, keepdims=True)
        weights = jnp.where(allowed[None, None, :], jnp.exp(scores - row_max), 0.0)
        row_total = jnp.sum(weights, axis=-1)
        probs = lax.optimization_barrier(weights.astype(jnp.bfloat16)).astype(jnp.float32)
        weighted = jnp.einsum("hqk,khd->qhd", probs, value_full)
        result = weighted / jnp.transpose(row_total)[:, :, None]
        return result.astype(jnp.bfloat16).reshape(TOK_DEV, heads_all * HD)

    attended = lax.map(one_slot, jnp.arange(N_TM, dtype=jnp.int32)).reshape(TOKENS, heads_all * HD)
    velocity = jnp.dot(attended, out_weight, preferred_element_type=jnp.float32)
    velocity = jnp.where(row_live[:, None], velocity, 0.0)
    updated = latents.astype(jnp.float32) + step_size[row_span][:, None] * velocity
    updated = updated.astype(jnp.bfloat16)
    slot_of_span = jnp.argsort(span_of_slot).astype(jnp.int32)
    by_span = updated.reshape(N_TM, TOK_DEV, LAT)[slot_of_span]
    by_span = by_span[:, decoder_order, :]
    denoised = jnp.transpose(by_span, (1, 0, 2))
    padded = jnp.pad(denoised.astype(jnp.float32), ((0, 0), (KT - 1, 0), (0, 0)))
    kernel = conv_weight.astype(jnp.float32)
    features = jnp.zeros((TOK_DEV, N_TM, COUT), jnp.float32)
    for shift_back in range(KT):
        window = padded[:, KT - 1 - shift_back:KT - 1 - shift_back + N_TM, :]
        features = features + jnp.einsum("ptf,fo->pto", window, kernel[shift_back])
    return denoised, features.astype(jnp.bfloat16)
```

```python
import jax
import jax.numpy as jnp
from jax import lax
from jax.experimental import pallas as pl
from jax.experimental.pallas import tpu as pltpu
from jax.sharding import PartitionSpec as P

HD = 128
HPD = 3
TOK = 128
LAT = 64
KT = 3
NX, NZ, NY = 4, 2, 8
NB = NX * NZ
NG = 8
PAIRS = TOK // 2
NSLOT = NB * NY
EXCLUDED = -1e30
SCALE = 1.4426950408889634 / HD**0.5
MESH = pl.DeviceIdType.MESH
QROWS = 256


def mod(value, size):
    return lax.rem(value + 2 * size, size)


def remote(src, dst, send, recv, device):
    return pltpu.make_async_remote_copy(
        src_ref=src, dst_ref=dst, send_sem=send, recv_sem=recv, device_id=device, device_id_type=MESH
    )


def kernel(
    q_ref, k_ref, v_ref, lat_ref, wout_ref, conv_ref, span_row_ref, order_ref,
    span_ref, valid_ref, step_ref,
    denoised_ref, features_ref,
    qbuf, kvbuf, vwbuf, obuf, lsebuf, sendbuf, c1buf, dbuf, ubuf, bias,
    q_send, q_recv, z_send, z_recv, x_send, x_recv, s_send, s_recv, c_send, c_recv, d_send, d_recv,
):
    tm = lax.axis_index("tm")
    g = lax.axis_index("head")
    b, a = lax.div(tm, NY), lax.rem(tm, NY)
    x, zh = lax.div(b, NZ), lax.rem(b, NZ)
    core = lax.rem(g, 2)
    way = 1 - 2 * core

    def slot_of(bb, aa):
        return bb * NY + aa

    y_next, y_prev = mod(a + way, NY), mod(a - way, NY)
    x_next, x_prev = mod(x + way, NX), mod(x - way, NX)
    to_y = {1: (slot_of(b, y_next), g), -1: (slot_of(b, y_prev), g)}
    to_x = {1: (slot_of(x_next * NZ + zh, a), g), -1: (slot_of(x_prev * NZ + zh, a), g)}
    b_other = x * NZ + 1 - zh
    to_z = (slot_of(b_other, a), g)
    self_last = b == g

    barrier = pltpu.get_barrier_semaphore()

    def greet(device):
        pl.semaphore_signal(barrier, inc=1, device_id=device, device_id_type=MESH)

    for device in (to_y[1], to_y[-1], to_x[1], to_x[-1], to_z):
        greet(device)
    for rel in range(1, NY * NG):
        greet((slot_of(b, mod(a + rel // NG, NY)), mod(g + rel % NG, NG)))
    for bb in range(NB):
        @pl.when(jnp.logical_not(jnp.logical_and(bb == b, self_last)))
        def _():
            greet((slot_of(bb, a), b))

    lane = lax.broadcasted_iota(jnp.int32, (TOK, TOK), 1)
    row = lax.broadcasted_iota(jnp.int32, (TOK, TOK), 0)
    order = order_ref[...].astype(jnp.float32)
    order_col = jnp.transpose(jnp.broadcast_to(order, (TOK, TOK)))
    pick = (order_col == lane.astype(jnp.float32)).astype(jnp.bfloat16)
    halves = (lane == 2 * lax.rem(row, PAIRS) + lax.div(row, PAIRS)).astype(jnp.bfloat16)
    pick = jnp.dot(halves, pick, preferred_element_type=jnp.float32).astype(jnp.bfloat16)
    order_row = lax.dot_general(
        jnp.broadcast_to(order, (8, TOK)).astype(jnp.bfloat16), halves, (((1,), (1,)), ((), ())),
        preferred_element_type=jnp.float32,
    )
    q_own = jnp.dot(pick, q_ref[...], preferred_element_type=jnp.float32).astype(jnp.bfloat16)
    for h in range(HPD):
        cols = slice(h * HD, (h + 1) * HD)
        qbuf[h, a] = q_own[:, cols]
        kvbuf[h, b, :TOK] = k_ref[:, cols]
        vw = jnp.dot(v_ref[:, cols], wout_ref[cols, :], preferred_element_type=jnp.float32)
        kvbuf[h, b, TOK:] = jnp.concatenate([vw[:PAIRS], vw[PAIRS:]], axis=1).astype(jnp.bfloat16)
    lat = jnp.dot(pick, lat_ref[...], preferred_element_type=jnp.float32)
    lat = jnp.concatenate([lat[:PAIRS], lat[PAIRS:]], axis=1)
    lat = jnp.where(g == 0, lat, 0.0)

    key_row = lax.broadcasted_iota(jnp.int32, (1, TOK), 1)
    my_spans = [span_ref[slot_of(b, i)] for i in range(NY)]
    for j in range(NB):
        key_span = span_ref[slot_of(j, a)]
        key_live = key_row < valid_ref[key_span]
        for i in range(NY):
            kept = jnp.logical_and(key_live, key_span <= my_spans[i])
            bias[i : i + 1, j * TOK : (j + 1) * TOK] = jnp.where(kept, 0.0, EXCLUDED)
    step_rows = jnp.concatenate(
        [
            jnp.where(order_row[0:1] < valid_ref[my_spans[i]].astype(jnp.float32), step_ref[my_spans[i]], 0.0)
            for i in range(NY)
        ],
        axis=0,
    )
    vwbuf[:, LAT:TOK] = jnp.zeros((NB * TOK, LAT), jnp.bfloat16)
    vwbuf[:, TOK:] = jnp.ones((NB * TOK, TOK), jnp.bfloat16)

    pl.semaphore_wait(barrier, 5 + NY * NG - 1 + NG - self_last.astype(jnp.int32))

    def q_copy(h, side, t):
        block = qbuf.at[h, mod(a - side * way * (t - 1), NY)]
        n = (0 if side == 1 else 4) + t - 1
        return remote(block, block, q_send.at[h, n], q_recv.at[h, n], to_y[side])

    def z_copy(h):
        block = kvbuf.at[h, b]
        return remote(block, block, z_send.at[h], z_recv.at[h], to_z)

    def x_copy(h, other, side, t):
        zz = 1 - zh if other else zh
        block = kvbuf.at[h, mod(x - side * way * (t - 1), NX) * NZ + zz]
        n = other * 3 + (0 if side == 1 else 2) + t - 1
        return remote(block, block, x_send.at[h, n], x_recv.at[h, n], to_x[side])

    started = []

    def start(copy):
        copy.start()
        started.append(copy)

    for h in range(HPD):
        start(z_copy(h))
        start(q_copy(h, 1, 1))
        start(q_copy(h, -1, 1))
        start(x_copy(h, 0, 1, 1))
        start(x_copy(h, 0, -1, 1))
    for h in range(HPD):
        q_copy(h, 1, 1).wait_recv()
        start(q_copy(h, 1, 2))
        q_copy(h, -1, 1).wait_recv()
        start(q_copy(h, -1, 2))
        x_copy(h, 0, 1, 1).wait_recv()
        start(x_copy(h, 0, 1, 2))
    for h in range(HPD):
        z_copy(h).wait_recv()
        start(x_copy(h, 1, 1, 1))
        start(x_copy(h, 1, -1, 1))
        q_copy(h, 1, 2).wait_recv()
        start(q_copy(h, 1, 3))
        q_copy(h, -1, 2).wait_recv()
        start(q_copy(h, -1, 3))
    for h in range(HPD):
        q_copy(h, 1, 3).wait_recv()
        start(q_copy(h, 1, 4))
        x_copy(h, 1, 1, 1).wait_recv()
        start(x_copy(h, 1, 1, 2))

    def lse_copy(h, rel):
        block = lsebuf.at[h, a]
        return remote(
            block, block, s_send.at[h, rel - 1], s_recv.at[h, rel - 1], (slot_of(b, mod(a + rel, NY)), g)
        )

    stat_lane = lax.broadcasted_iota(jnp.int32, (TOK, TOK), 1)
    for h in range(HPD):
        q_copy(h, 1, 4).wait_recv()
        q_copy(h, -1, 3).wait_recv()
        x_copy(h, 0, -1, 1).wait_recv()
        x_copy(h, 0, 1, 2).wait_recv()
        x_copy(h, 1, -1, 1).wait_recv()
        x_copy(h, 1, 1, 2).wait_recv()
        keys = kvbuf[h, :, :TOK].reshape(NB * TOK, HD)
        for j in range(NB):
            packed = kvbuf[h, j, TOK:]
            vwbuf[j * TOK : j * TOK + PAIRS, :LAT] = packed[:, :LAT]
            vwbuf[j * TOK + PAIRS : (j + 1) * TOK, :LAT] = packed[:, LAT:]
        vw = vwbuf[...]
        stats = jnp.zeros((TOK, TOK), jnp.float32)
        per = QROWS // TOK
        for i in range(NY // per):
            queries = qbuf[h, i * per : (i + 1) * per].reshape(QROWS, HD)
            scores = lax.dot_general(
                queries, keys, (((1,), (1,)), ((), ())), preferred_element_type=jnp.float32
            )
            scores = scores.reshape(per, TOK, NB * TOK) + bias[i * per : (i + 1) * per][:, None, :]
            scores = scores.reshape(QROWS, NB * TOK)
            top = jnp.max(scores, axis=1, keepdims=True)
            probs = jnp.exp2((scores - top) * SCALE).astype(jnp.bfloat16)
            out = jnp.dot(probs, vw, preferred_element_type=jnp.float32)
            total = out[:, TOK:]
            obuf[h, i * QROWS : (i + 1) * QROWS] = out[:, :TOK] / total
            lse = top * SCALE + jnp.log2(total)
            for p in range(per):
                stats = jnp.where(stat_lane == i * per + p, lse[p * TOK : (p + 1) * TOK], stats)
        lsebuf[h, a] = jnp.transpose(stats)[:NY]
        for rel in range(1, NY):
            start(lse_copy(h, rel))

    shares = []
    for h in range(HPD):
        for rel in range(1, NY):
            lse_copy(h, rel).wait_recv()
        parts = lsebuf[h]
        top = jnp.max(parts, axis=0)
        total = jnp.sum(jnp.exp2(parts - top[None]), axis=0)
        shares.append(jnp.exp2(lsebuf[h, a] - top) / total * step_rows)
    shares.append(jnp.zeros((TOK - HPD * NY, TOK), jnp.float32))
    share_cols = jnp.transpose(jnp.concatenate(shares, axis=0))
    terms = []
    for i in range(NY):
        rows = slice(i * TOK, (i + 1) * TOK)
        term = sum(obuf[h, rows] * share_cols[:, h * NY + i : h * NY + i + 1] for h in range(HPD))
        term = term[:PAIRS] + pltpu.roll(term[PAIRS:], LAT, 1)
        terms.append(term + jnp.where(a == i, lat, 0.0))
    sendbuf[...] = jnp.swapaxes(jnp.stack(terms, axis=0), 0, 1)

    def c_copy(rel):
        aa, gg = mod(a + rel // NG, NY), mod(g + rel % NG, NG)
        return remote(
            sendbuf.at[gg * NY + aa], c1buf.at[rel - 1], c_send, c_recv, (slot_of(b, aa), gg)
        )

    for rel in range(1, NY * NG):
        c_copy(rel).start()
    everything = remote(sendbuf.at[: NY * NG - 1], c1buf, c_send, c_recv, to_z)
    everything.wait_recv()
    ubuf[...] = sendbuf[g * NY + a] + jnp.sum(c1buf[...], axis=0)

    def d_copy(gg):
        return remote(ubuf, dbuf.at[b], d_send.at[gg], d_recv.at[b], (slot_of(g, a), gg))

    def own_target(gg):
        return jnp.logical_and(self_last, gg == g)

    for gg in range(NG):
        @pl.when(jnp.logical_not(own_target(gg)))
        def _():
            d_copy(gg).start()

    @pl.when(self_last)
    def _():
        dbuf[b] = ubuf[...]

    zeros = jnp.zeros((LAT, LAT), jnp.bfloat16)
    taps = []
    for k in range(KT):
        tap = conv_ref[k]
        taps.append(jnp.concatenate([tap, zeros], axis=1))
        taps.append(jnp.concatenate([zeros, tap], axis=1))
    taps = jnp.concatenate(taps, axis=0)
    time = lax.broadcasted_iota(jnp.int32, (NSLOT, NSLOT), 0)
    spans = jnp.broadcast_to(span_row_ref[...], (NSLOT, NSLOT))
    orders = [(spans == time - k).astype(jnp.bfloat16) for k in range(KT)]

    for bb in range(NB):
        @pl.when(jnp.logical_not(jnp.logical_and(self_last, bb == b)))
        def _():
            remote(ubuf, dbuf.at[bb], d_send.at[0], d_recv.at[bb], to_z).wait_recv()
    updated = dbuf[...].reshape(NSLOT, 2 * LAT).astype(jnp.bfloat16)
    shifted = [
        jnp.dot(order, updated, preferred_element_type=jnp.float32).astype(jnp.bfloat16) for order in orders
    ]
    features = jnp.dot(
        jnp.concatenate(shifted, axis=1), taps, preferred_element_type=jnp.float32
    ).astype(jnp.bfloat16)
    for p in range(2):
        denoised_ref[p] = shifted[0][:, p * LAT : (p + 1) * LAT]
        features_ref[p] = features[:, p * LAT : (p + 1) * LAT]

    for copy in started:
        copy.wait_send()
    everything.wait_send()
    for gg in range(NG):
        @pl.when(jnp.logical_not(own_target(gg)))
        def _():
            d_copy(gg).wait_send()


def local(
    queries, keys, values, latents, out_weight, step_size, conv_weight, span_of_slot, valid_count, decoder_order
):
    vmem, smem = pl.BlockSpec(memory_space=pltpu.VMEM), pl.BlockSpec(memory_space=pltpu.SMEM)
    dma = pltpu.SemaphoreType.DMA
    out = jax.ShapeDtypeStruct((2, NSLOT, LAT), jnp.bfloat16)
    return pl.pallas_call(
        kernel,
        out_shape=(out, out),
        in_specs=[vmem] * 8 + [smem] * 3,
        out_specs=(vmem, vmem),
        scratch_shapes=[
            pltpu.VMEM((HPD, NY, TOK, HD), jnp.bfloat16),
            pltpu.VMEM((HPD, NB, TOK + PAIRS, HD), jnp.bfloat16),
            pltpu.VMEM((NB * TOK, 2 * TOK), jnp.bfloat16),
            pltpu.VMEM((HPD, NY * TOK, TOK), jnp.float32),
            pltpu.VMEM((HPD, NY, NY, TOK), jnp.float32),
            pltpu.VMEM((PAIRS, NY, TOK), jnp.float32),
            pltpu.VMEM((NY * NG - 1, NY, TOK), jnp.float32),
            pltpu.VMEM((NB, NY, TOK), jnp.float32),
            pltpu.VMEM((NY, TOK), jnp.float32),
            pltpu.VMEM((NY, NB * TOK), jnp.float32),
            dma((HPD, 7)), dma((HPD, 7)),
            dma((HPD,)), dma((HPD,)),
            dma((HPD, 6)), dma((HPD, 6)),
            dma((HPD, NY - 1)), dma((HPD, NY - 1)),
            dma, dma,
            dma((NG,)), dma((NB,)),
        ],
        compiler_params=pltpu.CompilerParams(
            collective_id=0, has_side_effects=True, vmem_limit_bytes=48 * 2**20
        ),
        name="span_attention",
    )(
        queries, keys, values, latents, out_weight, conv_weight,
        span_of_slot.reshape(1, NSLOT), decoder_order.reshape(1, TOK),
        span_of_slot, valid_count, step_size,
    )


def solution(mesh):
    return jax.shard_map(
        local,
        mesh=mesh,
        in_specs=(
            P("tm", "head"),
            P("tm", "head"),
            P("tm", "head"),
            P("tm", None),
            P("head", None),
            P(),
            P(None, None, "head"),
            P(),
            P(),
            P(),
        ),
        out_specs=(P("tm", None, None), P("tm", None, "head")),
        check_vma=False,
    )
```

```python
import jax
import jax.numpy as jnp
from jax import lax
from jax.experimental import pallas as pl
from jax.experimental.pallas import tpu as pltpu
from jax.sharding import PartitionSpec as P

HD = 128
HPD = 3
TOK = 128
LAT = 64
KT = 3
NX, NZ, NY = 4, 2, 8
NB = NX * NZ
NG = 8
NL = NG // 2
PAIRS = TOK // 2
NSLOT = NB * NY
HALF = NX * TOK
EXCLUDED = -1e30
SCALE = 1.4426950408889634 / HD**0.5
MESH = pl.DeviceIdType.MESH
ROWS_BY_KEYS = (((1,), (1,)), ((), ()))


def mod(value, size):
    return lax.rem(value + 2 * size, size)


def remote(src, dst, send, recv, device):
    return pltpu.make_async_remote_copy(
        src_ref=src, dst_ref=dst, send_sem=send, recv_sem=recv, device_id=device, device_id_type=MESH
    )


def dot(left, right, dims=(((1,), (0,)), ((), ()))):
    return lax.dot_general(left, right, dims, preferred_element_type=jnp.float32)


def kernel(
    q_hbm, k_hbm, v_hbm, lat_hbm, wout_hbm, conv_hbm, span_row_hbm, order_hbm, span_hbm, valid_hbm, step_hbm,
    denoised_ref, features_ref,
    v_ref, lat_ref, wout_ref, conv_ref, span_row_ref, order_ref, span_ref, valid_ref, step_ref,
    qbuf, kvbuf, vwbuf, acc, tops, obuf, bias, lsebuf, sendbuf, pairbuf, c1buf, ubuf, dbuf,
    ready, load, q_send, q_recv, z_send, z_recv, x_send, x_recv, s_send, s_recv,
    p_send, p_recv, c_send, c_recv, d_send, d_recv,
):
    tm = lax.axis_index("tm")
    g = lax.axis_index("head")
    b, a = lax.div(tm, NY), lax.rem(tm, NY)
    x, zh = lax.div(b, NZ), lax.rem(b, NZ)
    zl, core = lax.div(g, 2), lax.rem(g, 2)
    way = 1 - 2 * core

    def slot_of(bb, aa):
        return bb * NY + aa

    to_y = {s: (slot_of(b, mod(a + s * way, NY)), g) for s in (1, -1)}
    to_x = {s: (slot_of(mod(x + s, NX) * NZ + zh, a), g) for s in (1, -1, 2)}
    to_z = (slot_of(x * NZ + 1 - zh, a), g)
    to_core = (tm, g + way)
    self_last = b == g

    barrier = pltpu.get_barrier_semaphore()
    head_peers = [(tm, mod(g + rel, NG)) for rel in range(1, NG)]
    greeted = [to_z, to_x[1], to_x[-1], to_x[2], to_y[1], to_y[-1], *head_peers]
    for device in greeted:
        pl.semaphore_signal(barrier, inc=1, device_id=device, device_id_type=MESH)

    def partner(rel):
        return mod(a + rel // NL, NY), mod(zl + rel % NL, NL) * 2 + core

    loads = []

    def fetch(src, dst):
        copy = pltpu.make_async_copy(src, dst, load.at[len(loads)])
        copy.start()
        loads.append(copy)

    def cols(h):
        return slice(h * HD, (h + 1) * HD)

    fetch(v_hbm, v_ref)
    fetch(wout_hbm, wout_ref)
    for h in range(HPD):
        fetch(k_hbm.at[:, cols(h)], kvbuf.at[h, zh, x, :TOK])
    for h in range(HPD):
        fetch(q_hbm.at[:, cols(h)], qbuf.at[h, a])
    early = len(loads)
    for src, dst in (
        (span_hbm, span_ref), (valid_hbm, valid_ref), (step_hbm, step_ref), (span_row_hbm, span_row_ref),
        (order_hbm, order_ref), (lat_hbm, lat_ref), (conv_hbm, conv_ref),
    ):
        fetch(src, dst)
    for copy in loads[:2]:
        copy.wait()
    for h in range(HPD):
        vw = dot(v_ref[:, cols(h)], wout_ref[:, cols(h)], ROWS_BY_KEYS)
        kvbuf[h, zh, x, TOK:] = jnp.concatenate([vw[:PAIRS], vw[PAIRS:]], axis=1).astype(jnp.bfloat16)
    for copy in loads[2:early]:
        copy.wait()

    pl.semaphore_wait(barrier, len(greeted))

    def q_copy(h, side, t):
        block = qbuf.at[h, mod(a - side * way * (t - 1), NY)]
        n = (0 if side == 1 else 4) + t - 1
        return remote(block, block, q_send.at[h, n], q_recv.at[h, n], to_y[side])

    def z_copy(h):
        block = kvbuf.at[h, zh, x]
        return remote(block, block, z_send.at[h], z_recv.at[h], to_z)

    def x_copy(h, other, step):
        block = kvbuf.at[h, 1 - zh if other else zh, x]
        n = 3 * other + (1, -1, 2).index(step)
        return remote(block, block, x_send.at[h, n], x_recv.at[h, n], to_x[step])

    started = []

    def start(copy):
        copy.start()
        started.append(copy)

    def q_pass(h, side, t):
        q_copy(h, side, t).wait_recv()
        start(q_copy(h, side, t + 1))

    def z_pass(h):
        z_copy(h).wait_recv()
        for step in (2, 1, -1):
            start(x_copy(h, 1, step))

    for h in range(HPD):
        start(z_copy(h))
    for h in range(HPD):
        start(q_copy(h, 1, 1))
        start(q_copy(h, -1, 1))
    for h in range(HPD):
        for step in (2, 1, -1):
            start(x_copy(h, 0, step))

    for copy in loads[early:]:
        copy.wait()
    rels = (0, -1, 1, -2, 2, -3, 3, -4)
    slots = [mod(a + rel * way, NY) for rel in rels]
    lane = lax.broadcasted_iota(jnp.int32, (TOK, TOK), 1)
    row = lax.broadcasted_iota(jnp.int32, (TOK, TOK), 0)
    tile_lane, tile_row = lane[:NY], row[:NY]

    def by_row(scalars):
        tile = jnp.full((NY, TOK), scalars[0])
        for i in range(1, NY):
            tile = jnp.where(tile_row == i, scalars[i], tile)
        return tile

    query_spans = by_row([span_ref[slot_of(b, slot)] for slot in slots])
    for half in range(NZ):
        for j in range(NX):
            key_span = span_ref[slot_of(j * NZ + (zh if half == 0 else 1 - zh), a)]
            live = jnp.where(key_span <= query_spans, valid_ref[key_span], 0)
            bias[half, :, j * TOK : (j + 1) * TOK] = jnp.where(tile_lane < live, 0.0, EXCLUDED)

    for h in range(HPD):
        q_pass(h, 1, 1)
        q_pass(h, -1, 1)

    vwbuf[:, :, :, TOK:] = jnp.ones((HPD, NZ, HALF, TOK), jnp.bfloat16)
    my_spans = [span_ref[slot_of(b, i)] for i in range(NY)]
    live = by_row([valid_ref[span] for span in my_spans])
    step_rows = jnp.where(tile_lane < live, by_row([step_ref[span] for span in my_spans]), 0.0)
    order = jnp.broadcast_to(order_ref[...].astype(jnp.float32), (TOK, TOK))
    pick = (jnp.transpose(order) == lane.astype(jnp.float32)).astype(jnp.bfloat16)
    halves = (lane == 2 * lax.rem(row, PAIRS) + lax.div(row, PAIRS)).astype(jnp.bfloat16)
    pick = dot(halves, pick)
    lat = dot(pick.astype(jnp.bfloat16), lat_ref[...], ROWS_BY_KEYS)
    lat = jnp.where(g == 0, jnp.concatenate([lat[:PAIRS], lat[PAIRS:]], axis=1), 0.0)

    for h in range(HPD):
        q_pass(h, 1, 2)
        q_pass(h, -1, 2)

    def load_vw(h, half):
        for j in range(NX):
            packed = kvbuf[h, zh if half == 0 else 1 - zh, j, TOK:]
            for part in range(2):
                rows = slice(j * TOK + part * PAIRS, j * TOK + (part + 1) * PAIRS)
                vw = packed[:, part * LAT : (part + 1) * LAT]
                vwbuf[h, half, rows, :TOK] = jnp.concatenate([vw, vw], axis=1)

    def scores_of(h, half, places, queries):
        keys = kvbuf[h, zh if half == 0 else 1 - zh, :, :TOK].reshape(HALF, HD)
        scores = dot(queries, keys, ROWS_BY_KEYS)
        return jnp.concatenate(
            [scores[i * TOK : (i + 1) * TOK] + bias[half, n : n + 1] for i, n in enumerate(places)], axis=0
        )

    def weigh(h, half, scores, top):
        return dot(jnp.exp2((scores - top) * SCALE).astype(jnp.bfloat16), vwbuf[h, half])

    def stacked(ref, h, places):
        return jnp.concatenate([ref[h, slots[n]] for n in places], axis=0)

    def row_max(scores):
        return jnp.max(scores, axis=1, keepdims=True)

    def attend_own(h, places):
        scores = scores_of(h, 0, places, stacked(qbuf, h, places))
        top = row_max(scores)
        out = weigh(h, 0, scores, top)
        for i, n in enumerate(places):
            acc[h, slots[n]] = out[i * TOK : (i + 1) * TOK]
            tops[h, slots[n]] = top[i * TOK : (i + 1) * TOK]

    def finish(h, places, top, out):
        total = out[:, TOK:]
        lse = top * SCALE + jnp.log2(total)
        out = (out[:, :TOK] / total).astype(jnp.bfloat16)
        for i, n in enumerate(places):
            obuf[h, slots[n]] = out[i * TOK : (i + 1) * TOK]
        return [lse[i * TOK : (i + 1) * TOK] for i in range(len(places))]

    def attend_others(h, places):
        scores = scores_of(h, 1, places, stacked(qbuf, h, places))
        before = stacked(tops, h, places)
        top = jnp.maximum(row_max(scores), before)
        out = weigh(h, 1, scores, top) + jnp.exp2((before - top) * SCALE) * stacked(acc, h, places)
        return finish(h, places, top, out)

    def attend_all(h, places):
        queries = stacked(qbuf, h, places)
        scores = [scores_of(h, half, places, queries) for half in range(NZ)]
        top = jnp.maximum(row_max(scores[0]), row_max(scores[1]))
        return finish(h, places, top, sum(weigh(h, half, scores[half], top) for half in range(NZ)))

    def lse_copy(h, rel):
        block = lsebuf.at[h, a]
        return remote(block, block, s_send.at[h], s_recv.at[h], (slot_of(b, mod(a + rel, NY)), g))

    def lse_all(h):
        block = lsebuf.at[h, : NY - 1]
        return remote(block, block, s_send.at[h], s_recv.at[h], to_y[1])

    def lse_send(h, columns, lanes):
        stats = jnp.zeros((TOK, TOK), jnp.float32)
        for column, index in zip(columns, lanes):
            stats = jnp.where(lane == index, column, stats)
        lsebuf[h, a] = jnp.transpose(stats)[:NY]
        for rel in (4, 3, 5, 2, 6, 1, 7):
            lse_copy(h, rel).start()

    for h in range(HPD):
        for step in (1, -1, 2):
            x_copy(h, 0, step).wait_recv()
        load_vw(h, 0)
        attend_own(h, (0, 1, 2))
        if h == 0:
            z_pass(0)
    for h in range(HPD):
        attend_own(h, (3, 4))
        if h == 0:
            z_pass(1)
    z_pass(2)
    for h in range(HPD):
        q_pass(h, 1, 3)
        q_copy(h, -1, 3).wait_recv()
    for h in range(HPD):
        attend_own(h, (5, 6))
    for h in range(HPD):
        for step in (1, -1, 2):
            x_copy(h, 1, step).wait_recv()
        load_vw(h, 1)
        columns = attend_others(h, (0, 1, 2, 3)) + attend_others(h, (4, 5, 6))
        lse_send(h, columns, slots[: NY - 1])
    columns = []
    for h in range(HPD):
        q_copy(h, 1, 4).wait_recv()
        columns += attend_all(h, (NY - 1,))
    lse_send(HPD, columns, range(HPD))

    for device in head_peers:
        pl.semaphore_signal(ready, inc=1, device_id=device, device_id_type=MESH)

    for h in range(HPD + 1):
        lse_all(h).wait_recv()
    shares = []
    for h in range(HPD):
        parts = [
            jnp.where(tile_row == (i + NY // 2) % NY, lsebuf[HPD, i, h : h + 1], lsebuf[h, i]) for i in range(NY)
        ]
        own = jnp.where(tile_row == mod(a + NY // 2, NY), lsebuf[HPD, a, h : h + 1], lsebuf[h, a])
        top = parts[0]
        for part in parts[1:]:
            top = jnp.maximum(top, part)
        total = sum(jnp.exp2(part - top) for part in parts)
        shares.append(jnp.exp2(own - top) / total * step_rows)
    for i in range(NY):
        left = jnp.concatenate([(pick * share[i : i + 1]).astype(jnp.bfloat16) for share in shares], axis=1)
        term = dot(left, jnp.concatenate([obuf[h, i] for h in range(HPD)], axis=0))
        term = jnp.where(lane[:PAIRS] < LAT, term[:PAIRS], term[PAIRS:]) + jnp.where(a == i, lat, 0.0)
        for gg in range(NG):
            sendbuf[gg % 2, gg // 2, pl.ds(i, NY, stride=NY)] = term[gg * NY : (gg + 1) * NY]

    pl.semaphore_wait(ready, len(head_peers))
    pair_copy = remote(sendbuf.at[1 - core], pairbuf, p_send, p_recv, to_core)
    pair_copy.start()
    pair_copy.wait_recv()
    pairbuf[...] = pairbuf[...] + sendbuf[core]

    def owner(aa):
        return pl.ds(pl.multiple_of(aa * NY, NY), NY)

    def c_copy(rel):
        aa, gg = partner(rel)
        return remote(pairbuf.at[lax.div(gg, 2), owner(aa)], c1buf.at[rel - 1], c_send, c_recv, (slot_of(b, aa), gg))

    for rel in range(1, NY * NL):
        c_copy(rel).start()
    sums = remote(c1buf, c1buf, c_send, c_recv, to_core)
    sums.wait_recv()
    ubuf[...] = pairbuf[zl, owner(a)] + jnp.sum(c1buf[...], axis=0)

    def d_copy(gg):
        return remote(ubuf, dbuf.at[b], d_send.at[gg], d_recv.at[b], (slot_of(g, a), gg))

    def own_target(gg):
        return jnp.logical_and(self_last, gg == g)

    for gg in range(NG):
        @pl.when(jnp.logical_not(own_target(gg)))
        def _():
            d_copy(gg).start()

    @pl.when(self_last)
    def _():
        dbuf[b] = ubuf[...]

    zeros = jnp.zeros((LAT, LAT), jnp.bfloat16)
    taps = []
    for k in range(KT):
        tap = conv_ref[k]
        taps.append(jnp.concatenate([tap, zeros], axis=1))
        taps.append(jnp.concatenate([zeros, tap], axis=1))
    taps = jnp.concatenate(taps, axis=0)
    time = lax.broadcasted_iota(jnp.int32, (NSLOT, NSLOT), 0)
    spans = jnp.broadcast_to(span_row_ref[...], (NSLOT, NSLOT))
    orders = [(spans == time - k).astype(jnp.bfloat16) for k in range(KT)]

    for copy in started:
        copy.wait_send()
    for h in range(HPD + 1):
        lse_all(h).wait_send()
    pair_copy.wait_send()
    sums.wait_send()

    for bb in range(NB):
        @pl.when(jnp.logical_not(jnp.logical_and(self_last, bb == b)))
        def _():
            remote(ubuf, dbuf.at[bb], d_send.at[0], d_recv.at[bb], to_z).wait_recv()
    updated = dbuf[...].reshape(NSLOT, 2 * LAT).astype(jnp.bfloat16)
    shifted = [dot(order, updated).astype(jnp.bfloat16) for order in orders]
    features = dot(jnp.concatenate(shifted, axis=1), taps).astype(jnp.bfloat16)
    for p in range(2):
        denoised_ref[p] = shifted[0][:, p * LAT : (p + 1) * LAT]
        features_ref[p] = features[:, p * LAT : (p + 1) * LAT]

    for gg in range(NG):
        @pl.when(jnp.logical_not(own_target(gg)))
        def _():
            d_copy(gg).wait_send()


def local(
    queries, keys, values, latents, out_weight, step_size, conv_weight, span_of_slot, valid_count, decoder_order
):
    vmem, anywhere = pl.BlockSpec(memory_space=pltpu.VMEM), pl.BlockSpec(memory_space=pl.ANY)
    dma = pltpu.SemaphoreType.DMA
    bf16, f32, i32 = jnp.bfloat16, jnp.float32, jnp.int32
    out = jax.ShapeDtypeStruct((2, NSLOT, LAT), bf16)
    return pl.pallas_call(
        kernel,
        out_shape=(out, out),
        in_specs=[anywhere] * 11,
        out_specs=(vmem, vmem),
        scratch_shapes=[
            pltpu.VMEM((TOK, HPD * HD), bf16),
            pltpu.VMEM((LAT, TOK), bf16),
            pltpu.VMEM((LAT, HPD * HD), bf16),
            pltpu.VMEM((KT, LAT, LAT), bf16),
            pltpu.VMEM((1, NSLOT), i32),
            pltpu.VMEM((1, TOK), i32),
            pltpu.SMEM((NSLOT,), i32),
            pltpu.SMEM((NSLOT,), i32),
            pltpu.SMEM((NSLOT,), f32),
            pltpu.VMEM((HPD, NY, TOK, HD), bf16),
            pltpu.VMEM((HPD, NZ, NX, TOK + PAIRS, HD), bf16),
            pltpu.VMEM((HPD, NZ, HALF, 2 * TOK), bf16),
            pltpu.VMEM((HPD, NY, TOK, 2 * TOK), f32),
            pltpu.VMEM((HPD, NY, TOK, 1), f32),
            pltpu.VMEM((HPD, NY, TOK, TOK), bf16),
            pltpu.VMEM((NZ, NY, HALF), f32),
            pltpu.VMEM((HPD + 1, NY, NY, TOK), f32),
            pltpu.VMEM((2, NL, NY * NY, TOK), f32),
            pltpu.VMEM((NL, NY * NY, TOK), f32),
            pltpu.VMEM((NY * NL - 1, NY, TOK), f32),
            pltpu.VMEM((NY, TOK), f32),
            pltpu.VMEM((NB, NY, TOK), f32),
            pltpu.SemaphoreType.REGULAR,
            dma((15,)),
            dma((HPD, 7)), dma((HPD, 7)),
            dma((HPD,)), dma((HPD,)),
            dma((HPD, 6)), dma((HPD, 6)),
            dma((HPD + 1,)), dma((HPD + 1,)),
            dma, dma,
            dma, dma,
            dma((NG,)), dma((NB,)),
        ],
        compiler_params=pltpu.CompilerParams(
            collective_id=0, has_side_effects=True, vmem_limit_bytes=54 * 2**20
        ),
        name="span_attention",
    )(
        queries, keys, values, latents.T, out_weight.T, conv_weight,
        span_of_slot.reshape(1, NSLOT), decoder_order.reshape(1, TOK),
        span_of_slot, valid_count, step_size,
    )


def solution(mesh):
    return jax.shard_map(
        local,
        mesh=mesh,
        in_specs=(
            P("tm", "head"),
            P("tm", "head"),
            P("tm", "head"),
            P("tm", None),
            P("head", None),
            P(),
            P(None, None, "head"),
            P(),
            P(),
            P(),
        ),
        out_specs=(P("tm", None, None), P("tm", None, "head")),
        check_vma=False,
    )
```

```python
import jax
import jax.numpy as jnp
from jax import lax
from jax.experimental import pallas as pl
from jax.experimental.pallas import tpu as pltpu
from jax.sharding import PartitionSpec as P

HD = 128
HPD = 3
TOK = 128
LAT = 64
KT = 3
NX, NZ, NY = 4, 2, 8
NB = NX * NZ
NG = 8
NL = NG // 2
PAIRS = TOK // 2
NSLOT = NB * NY
HALF = NX * TOK
EXCLUDED = -1e30
SCALE = 1.4426950408889634 / HD**0.5
MESH = pl.DeviceIdType.MESH
ROWS_BY_KEYS = (((1,), (1,)), ((), ()))


def mod(value, size):
    return lax.rem(value + 2 * size, size)


def remote(src, dst, send, recv, device):
    return pltpu.make_async_remote_copy(
        src_ref=src, dst_ref=dst, send_sem=send, recv_sem=recv, device_id=device, device_id_type=MESH
    )


def dot(left, right, dims=(((1,), (0,)), ((), ()))):
    return lax.dot_general(left, right, dims, preferred_element_type=jnp.float32)


def kernel(
    q_hbm, k_hbm, v_hbm, lat_hbm, wout_hbm, conv_hbm, span_row_hbm, order_hbm, span_hbm, valid_hbm, step_hbm,
    out_ref,
    v_ref, lat_ref, wout_ref, conv_ref, span_row_ref, order_ref, span_ref, valid_ref, step_ref,
    qbuf, kvbuf, vwbuf, acc, tops, obuf, bias, lsebuf, stage, sendbuf, c1buf, sumbuf, pairbuf, ubuf, dbuf,
    ready, load, q_send, q_recv, z_send, z_recv, x_send, x_recv, s_send, s_recv,
    p_send, p_recv, c_send, c_recv, d_send, d_recv,
):
    tm = lax.axis_index("tm")
    g = lax.axis_index("head")
    b, a = lax.div(tm, NY), lax.rem(tm, NY)
    x, zh = lax.div(b, NZ), lax.rem(b, NZ)
    zl, core = lax.div(g, 2), lax.rem(g, 2)
    way = 1 - 2 * core

    def slot_of(bb, aa):
        return bb * NY + aa

    to_y = {s: (slot_of(b, mod(a + s * way, NY)), g) for s in (1, -1, 2, -2)}
    to_x = {s: (slot_of(mod(x + s, NX) * NZ + zh, a), g) for s in (1, -1, 2)}
    to_z = (slot_of(x * NZ + 1 - zh, a), g)
    to_core = (tm, g + way)
    self_last = b == g

    barrier = pltpu.get_barrier_semaphore()
    head_peers = [(tm, mod(g + rel, NG)) for rel in range(1, NG)]
    greeted = [to_z, to_x[1], to_x[-1], to_x[2], *to_y.values(), *head_peers]
    for device in greeted:
        pl.semaphore_signal(barrier, inc=1, device_id=device, device_id_type=MESH)

    def partner(rel):
        return mod(a + rel // NL, NY), mod(zl + rel % NL, NL) * 2 + core

    loads = []

    def fetch(src, dst):
        copy = pltpu.make_async_copy(src, dst, load.at[len(loads)])
        copy.start()
        loads.append(copy)

    def cols(h):
        return slice(h * HD, (h + 1) * HD)

    fetch(v_hbm, v_ref)
    fetch(wout_hbm, wout_ref)
    for h in range(HPD):
        fetch(k_hbm.at[:, cols(h)], kvbuf.at[h, zh, x, :TOK])
    for h in range(HPD):
        fetch(q_hbm.at[:, cols(h)], qbuf.at[h, a])
    early = len(loads)
    for src, dst in (
        (span_hbm, span_ref), (valid_hbm, valid_ref), (step_hbm, step_ref), (span_row_hbm, span_row_ref),
        (order_hbm, order_ref), (lat_hbm, lat_ref), (conv_hbm, conv_ref),
    ):
        fetch(src, dst)
    for copy in loads[:2]:
        copy.wait()
    for h in range(HPD):
        vw = dot(v_ref[:, cols(h)], wout_ref[:, cols(h)], ROWS_BY_KEYS)
        kvbuf[h, zh, x, TOK:] = jnp.concatenate([vw[:PAIRS], vw[PAIRS:]], axis=1).astype(jnp.bfloat16)
    for copy in loads[2:early]:
        copy.wait()

    pl.semaphore_wait(barrier, len(greeted))

    def q_copy(h, side, distance, hop):
        block = qbuf.at[h, mod(a - side * way * (distance - hop), NY)]
        n = (0 if side == 1 else 4) + distance - 1
        return remote(block, block, q_send.at[h, n], q_recv.at[h, n], to_y[side * hop])

    def q_wait(h, side, distance):
        q_copy(h, side, distance, min(distance, 2)).wait_recv()

    def z_copy(h):
        block = kvbuf.at[h, zh, x]
        return remote(block, block, z_send.at[h], z_recv.at[h], to_z)

    def x_copy(h, other, step):
        block = kvbuf.at[h, 1 - zh, x] if other else kvbuf.at[:, zh, x]
        n = 3 * other + (1, -1, 2).index(step)
        return remote(block, block, x_send.at[h, n], x_recv.at[h, n], to_x[step])

    started = []

    def start(copy):
        copy.start()
        started.append(copy)

    def q_pass(h):
        q_wait(h, 1, 2)
        start(q_copy(h, 1, 4, 2))
        start(q_copy(h, 1, 3, 1))
        q_wait(h, -1, 2)
        start(q_copy(h, -1, 3, 1))

    def z_pass(h):
        z_copy(h).wait_recv()
        for step in (2, 1, -1):
            start(x_copy(h, 1, step))

    for h in range(HPD):
        start(z_copy(h))
    for h in range(HPD):
        for side in (1, -1):
            start(q_copy(h, side, 2, 2))
    for step in (2, 1, -1):
        start(x_copy(0, 0, step))
    for h in range(HPD):
        for side in (1, -1):
            start(q_copy(h, side, 1, 1))

    for copy in loads[early:]:
        copy.wait()
    rels = (0, -1, 1, -2, 2, -3, 3, -4)
    slots = [mod(a + rel * way, NY) for rel in rels]
    lane = lax.broadcasted_iota(jnp.int32, (TOK, TOK), 1)
    row = lax.broadcasted_iota(jnp.int32, (TOK, TOK), 0)
    tile_lane, tile_row = lane[:NY], row[:NY]

    def by_row(scalars):
        tile = jnp.full((NY, TOK), scalars[0])
        for i in range(1, NY):
            tile = jnp.where(tile_row == i, scalars[i], tile)
        return tile

    query_spans = by_row([span_ref[slot_of(b, slot)] for slot in slots])
    for half in range(NZ):
        for j in range(NX):
            key_span = span_ref[slot_of(j * NZ + (zh if half == 0 else 1 - zh), a)]
            live = jnp.where(key_span <= query_spans, valid_ref[key_span], 0)
            bias[half, :, j * TOK : (j + 1) * TOK] = jnp.where(tile_lane < live, 0.0, EXCLUDED)

    vwbuf[:, :, :, TOK:] = jnp.ones((HPD, NZ, HALF, TOK), jnp.bfloat16)
    my_spans = [span_ref[slot_of(b, i)] for i in range(NY)]
    live = by_row([valid_ref[span] for span in my_spans])
    step_rows = jnp.where(tile_lane < live, by_row([step_ref[span] for span in my_spans]), 0.0)
    order = jnp.broadcast_to(order_ref[...].astype(jnp.float32), (TOK, TOK))
    pick = (jnp.transpose(order) == lane.astype(jnp.float32)).astype(jnp.bfloat16)
    halves = (lane == 2 * lax.rem(row, PAIRS) + lax.div(row, PAIRS)).astype(jnp.bfloat16)
    pick = dot(halves, pick)
    lat = dot(pick.astype(jnp.bfloat16), lat_ref[...], ROWS_BY_KEYS)
    lat = jnp.where(g == 0, jnp.concatenate([lat[:PAIRS], lat[PAIRS:]], axis=1), 0.0)

    for h in range(HPD):
        q_pass(h)
    for h in range(HPD):
        z_pass(h)

    def load_vw(h, half):
        for j in range(NX):
            packed = kvbuf[h, zh if half == 0 else 1 - zh, j, TOK:]
            for part in range(2):
                rows = slice(j * TOK + part * PAIRS, j * TOK + (part + 1) * PAIRS)
                vw = packed[:, part * LAT : (part + 1) * LAT]
                vwbuf[h, half, rows, :TOK] = jnp.concatenate([vw, vw], axis=1)

    def scores_of(h, half, places, queries):
        keys = kvbuf[h, zh if half == 0 else 1 - zh, :, :TOK].reshape(HALF, HD)
        scores = dot(queries, keys, ROWS_BY_KEYS)
        return jnp.concatenate(
            [scores[i * TOK : (i + 1) * TOK] + bias[half, n : n + 1] for i, n in enumerate(places)], axis=0
        )

    def weigh(h, half, scores, top):
        return dot(jnp.exp2((scores - top) * SCALE).astype(jnp.bfloat16), vwbuf[h, half])

    def stacked(ref, h, places):
        return jnp.concatenate([ref[h, slots[n]] for n in places], axis=0)

    def row_max(scores):
        return jnp.max(scores, axis=1, keepdims=True)

    def attend_own(h, places):
        scores = scores_of(h, 0, places, stacked(qbuf, h, places))
        top = row_max(scores)
        out = weigh(h, 0, scores, top)
        for i, n in enumerate(places):
            acc[h, slots[n]] = out[i * TOK : (i + 1) * TOK]
            tops[h, slots[n]] = top[i * TOK : (i + 1) * TOK]

    def finish(h, places, top, out):
        total = out[:, TOK:]
        lse = top * SCALE + jnp.log2(total)
        out = (out[:, :TOK] / total).astype(jnp.bfloat16)
        for i, n in enumerate(places):
            obuf[h, slots[n]] = out[i * TOK : (i + 1) * TOK]
        return [lse[i * TOK : (i + 1) * TOK] for i in range(len(places))]

    def attend_others(h, places):
        scores = scores_of(h, 1, places, stacked(qbuf, h, places))
        before = stacked(tops, h, places)
        top = jnp.maximum(row_max(scores), before)
        out = weigh(h, 1, scores, top) + jnp.exp2((before - top) * SCALE) * stacked(acc, h, places)
        return finish(h, places, top, out)

    def attend_all(h, places):
        queries = stacked(qbuf, h, places)
        scores = [scores_of(h, half, places, queries) for half in range(NZ)]
        top = jnp.maximum(row_max(scores[0]), row_max(scores[1]))
        return finish(h, places, top, sum(weigh(h, half, scores[half], top) for half in range(NZ)))

    def lse_copy(h, rel):
        block = lsebuf.at[h, a]
        return remote(block, block, s_send.at[h], s_recv.at[h], (slot_of(b, mod(a + rel, NY)), g))

    def lse_all(h):
        block = lsebuf.at[h, : NY - 1]
        return remote(block, block, s_send.at[h], s_recv.at[h], to_y[1])

    def lse_send(h, columns, places):
        stats = jnp.zeros((TOK, TOK), jnp.float32)
        for column, index in zip(columns, [slots[n] for n in places]):
            stats = jnp.where(lane == index, column, stats)
        lsebuf[h, a] = jnp.transpose(stats)[:NY]
        for rel in (4, 3, 5, 2, 6, 1, 7):
            lse_copy(h, rel).start()

    for step in (1, -1, 2):
        x_copy(0, 0, step).wait_recv()
    for h in range(HPD):
        load_vw(h, 0)
        q_wait(h, 1, 1)
        q_wait(h, -1, 1)
        attend_own(h, (0, 1, 2))
        attend_own(h, (3, 4))
    for h in range(HPD):
        q_wait(h, 1, 3)
        q_wait(h, -1, 3)
        q_wait(h, 1, 4)
    for h in range(HPD):
        attend_own(h, (5, 6, 7))
    for h in range(HPD):
        for step in (1, -1, 2):
            x_copy(h, 1, step).wait_recv()
        load_vw(h, 1)
        columns = attend_others(h, (0, 1, 2, 3)) + attend_others(h, (4, 5, 6, 7))
        lse_send(h, columns, range(NY))

    for device in head_peers:
        pl.semaphore_signal(ready, inc=1, device_id=device, device_id_type=MESH)

    for h in range(HPD):
        lse_all(h).wait_recv()
    shares = []
    for h in range(HPD):
        parts = lsebuf[h]
        top = jnp.max(parts, axis=0)
        total = jnp.sum(jnp.exp2(parts - top[None]), axis=0)
        shares.append(jnp.exp2(lsebuf[h, a] - top) / total * step_rows)
    for i in range(NY):
        left = jnp.concatenate([(pick * share[i : i + 1]).astype(jnp.bfloat16) for share in shares], axis=1)
        term = dot(left, jnp.concatenate([obuf[h, i] for h in range(HPD)], axis=0))
        term = jnp.where(lane[:PAIRS] < LAT, term[:PAIRS], term[PAIRS:]) + jnp.where(a == i, lat, 0.0)
        for gg in range(NG):
            stage[gg // 2, pl.ds(gg % 2 * NY + i, NY, stride=2 * NY)] = term[gg * NY : (gg + 1) * NY]
    sendbuf[...] = stage[...].astype(jnp.bfloat16)

    pl.semaphore_wait(ready, len(head_peers))

    def owner(aa):
        return pl.ds(pl.multiple_of(aa * 2 * NY, 2 * NY), 2 * NY)

    def c_copy(rel):
        aa, gg = partner(rel)
        return remote(sendbuf.at[lax.div(gg, 2), owner(aa)], c1buf.at[rel - 1], c_send, c_recv, (slot_of(b, aa), gg))

    def hops(rel):
        return min(rel // NL, NY - rel // NL) + min(rel % NL, NL - rel % NL)

    for rel in sorted(range(1, NY * NL), key=hops, reverse=True):
        c_copy(rel).start()
    sums = remote(c1buf, c1buf, c_send, c_recv, to_core)
    sums.wait_recv()
    total = stage[zl, owner(a)] + jnp.sum(c1buf[...].astype(jnp.float32), axis=0)
    sumbuf[...] = total.reshape(2, NY, TOK)
    pair_copy = remote(sumbuf.at[1 - core], pairbuf, p_send, p_recv, to_core)
    pair_copy.start()
    pair_copy.wait_recv()
    ubuf[...] = sumbuf[core] + pairbuf[...]

    def d_copy(gg):
        return remote(ubuf, dbuf.at[b], d_send.at[gg], d_recv.at[b], (slot_of(g, a), gg))

    def own_target(gg):
        return jnp.logical_and(self_last, gg == g)

    for gg in range(NG):
        @pl.when(jnp.logical_not(own_target(gg)))
        def _():
            d_copy(gg).start()

    @pl.when(self_last)
    def _():
        dbuf[b] = ubuf[...]

    zeros = jnp.zeros((LAT, LAT), jnp.bfloat16)
    taps = []
    for k in range(KT):
        tap = conv_ref[k]
        taps.append(jnp.concatenate([tap, zeros], axis=1))
        taps.append(jnp.concatenate([zeros, tap], axis=1))
    taps = jnp.concatenate(taps, axis=0)
    time = lax.broadcasted_iota(jnp.int32, (NSLOT, NSLOT), 0)
    spans = jnp.broadcast_to(span_row_ref[...], (NSLOT, NSLOT))
    orders = [(spans == time - k).astype(jnp.bfloat16) for k in range(KT)]

    for copy in started:
        copy.wait_send()
    for h in range(HPD):
        lse_all(h).wait_send()
    pair_copy.wait_send()
    sums.wait_send()

    for bb in range(NB):
        @pl.when(jnp.logical_not(jnp.logical_and(self_last, bb == b)))
        def _():
            remote(ubuf, dbuf.at[bb], d_send.at[0], d_recv.at[bb], to_z).wait_recv()
    updated = dbuf[...].reshape(NSLOT, 2 * LAT).astype(jnp.bfloat16)
    shifted = [dot(order, updated).astype(jnp.bfloat16) for order in orders]
    features = dot(jnp.concatenate(shifted, axis=1), taps).astype(jnp.bfloat16)
    denoised = shifted[0]
    for p in range(2):
        part = slice(p * LAT, (p + 1) * LAT)
        out_ref[p] = jnp.concatenate([denoised[:, part], features[:, part]], axis=1)

    for gg in range(NG):
        @pl.when(jnp.logical_not(own_target(gg)))
        def _():
            d_copy(gg).wait_send()


def local(
    queries, keys, values, latents, out_weight, step_size, conv_weight, span_of_slot, valid_count, decoder_order
):
    vmem, anywhere = pl.BlockSpec(memory_space=pltpu.VMEM), pl.BlockSpec(memory_space=pl.ANY)
    dma = pltpu.SemaphoreType.DMA
    bf16, f32, i32 = jnp.bfloat16, jnp.float32, jnp.int32
    both = pl.pallas_call(
        kernel,
        out_shape=jax.ShapeDtypeStruct((2, NSLOT, 2 * LAT), bf16),
        in_specs=[anywhere] * 11,
        out_specs=vmem,
        scratch_shapes=[
            pltpu.VMEM((TOK, HPD * HD), bf16),
            pltpu.VMEM((LAT, TOK), bf16),
            pltpu.VMEM((LAT, HPD * HD), bf16),
            pltpu.VMEM((KT, LAT, LAT), bf16),
            pltpu.VMEM((1, NSLOT), i32),
            pltpu.VMEM((1, TOK), i32),
            pltpu.SMEM((NSLOT,), i32),
            pltpu.SMEM((NSLOT,), i32),
            pltpu.SMEM((NSLOT,), f32),
            pltpu.VMEM((HPD, NY, TOK, HD), bf16),
            pltpu.VMEM((HPD, NZ, NX, TOK + PAIRS, HD), bf16),
            pltpu.VMEM((HPD, NZ, HALF, 2 * TOK), bf16),
            pltpu.VMEM((HPD, NY, TOK, 2 * TOK), f32),
            pltpu.VMEM((HPD, NY, TOK, 1), f32),
            pltpu.VMEM((HPD, NY, TOK, TOK), bf16),
            pltpu.VMEM((NZ, NY, HALF), f32),
            pltpu.VMEM((HPD, NY, NY, TOK), f32),
            pltpu.VMEM((NL, 2 * NY * NY, TOK), f32),
            pltpu.VMEM((NL, 2 * NY * NY, TOK), bf16),
            pltpu.VMEM((NY * NL - 1, 2 * NY, TOK), bf16),
            pltpu.VMEM((2, NY, TOK), f32),
            pltpu.VMEM((NY, TOK), f32),
            pltpu.VMEM((NY, TOK), f32),
            pltpu.VMEM((NB, NY, TOK), f32),
            pltpu.SemaphoreType.REGULAR,
            dma((15,)),
            dma((HPD, 7)), dma((HPD, 7)),
            dma((HPD,)), dma((HPD,)),
            dma((HPD, 6)), dma((HPD, 6)),
            dma((HPD,)), dma((HPD,)),
            dma, dma,
            dma, dma,
            dma((NG,)), dma((NB,)),
        ],
        compiler_params=pltpu.CompilerParams(
            collective_id=0, has_side_effects=True, vmem_limit_bytes=54 * 2**20
        ),
        name="span_attention",
    )(
        queries, keys, values, latents.T, out_weight.T, conv_weight,
        span_of_slot.reshape(1, NSLOT), decoder_order.reshape(1, TOK),
        span_of_slot, valid_count, step_size,
    )
    return both[:, :, :LAT], both[:, :, LAT:]


def solution(mesh):
    return jax.shard_map(
        local,
        mesh=mesh,
        in_specs=(
            P("tm", "head"),
            P("tm", "head"),
            P("tm", "head"),
            P("tm", None),
            P("head", None),
            P(),
            P(None, None, "head"),
            P(),
            P(),
            P(),
        ),
        out_specs=(P("tm", None, None), P("tm", None, "head")),
        check_vma=False,
    )
```

```python
import jax
import jax.numpy as jnp
from jax import lax
from jax.experimental import pallas as pl
from jax.experimental.pallas import tpu as pltpu
from jax.sharding import PartitionSpec as P

HD = 128
HPD = 3
TOK = 128
LAT = 64
KT = 3
NX, NZ, NY = 4, 2, 8
NB = NX * NZ
NG = 8
NL = NG // 2
PAIRS = TOK // 2
NSLOT = NB * NY
HALF = NX * TOK
EXCLUDED = -1e30
SCALE = 1.4426950408889634 / HD**0.5
MESH = pl.DeviceIdType.MESH
ROWS_BY_KEYS = (((1,), (1,)), ((), ()))


def mod(value, size):
    return lax.rem(value + 2 * size, size)


def remote(src, dst, send, recv, device):
    return pltpu.make_async_remote_copy(
        src_ref=src, dst_ref=dst, send_sem=send, recv_sem=recv, device_id=device, device_id_type=MESH
    )


def dot(left, right, dims=(((1,), (0,)), ((), ()))):
    return lax.dot_general(left, right, dims, preferred_element_type=jnp.float32)


def kernel(
    q_hbm, k_hbm, v_hbm, lat_hbm, wout_hbm, conv_hbm, span_row_hbm, order_hbm, span_hbm, valid_hbm, step_hbm,
    out_ref,
    v_ref, lat_ref, wout_ref, conv_ref, span_row_ref, order_ref, span_ref, valid_ref, step_ref,
    qbuf, kvbuf, vwbuf, acc, tops, obuf, bias, lsebuf, stage, sendbuf, c1buf, sumbuf, pairbuf, ubuf, dbuf,
    ready, load, q_send, q_recv, z_send, z_recv, x_send, x_recv, s_send, s_recv,
    p_send, p_recv, c_send, c_recv, d_send, d_recv,
):
    tm = lax.axis_index("tm")
    g = lax.axis_index("head")
    b, a = lax.div(tm, NY), lax.rem(tm, NY)
    x, zh = lax.div(b, NZ), lax.rem(b, NZ)
    zl, core = lax.div(g, 2), lax.rem(g, 2)
    way = 1 - 2 * core

    def slot_of(bb, aa):
        return bb * NY + aa

    to_y = {s: (slot_of(b, mod(a + s * way, NY)), g) for s in (1, -1, 2, -2)}
    to_x = {s: (slot_of(mod(x + s, NX) * NZ + zh, a), g) for s in (1, -1, 2)}
    to_z = (slot_of(x * NZ + 1 - zh, a), g)
    to_core = (tm, g + way)
    self_last = b == g

    barrier = pltpu.get_barrier_semaphore()
    head_peers = [(tm, mod(g + rel, NG)) for rel in range(1, NG)]
    greeted = [to_z, to_x[1], to_x[-1], to_x[2], *to_y.values(), *head_peers]
    for device in greeted:
        pl.semaphore_signal(barrier, inc=1, device_id=device, device_id_type=MESH)

    def partner(rel):
        return mod(a + rel // NL, NY), mod(zl + rel % NL, NL) * 2 + core

    loads = []

    def fetch(src, dst):
        copy = pltpu.make_async_copy(src, dst, load.at[len(loads)])
        copy.start()
        loads.append(copy)

    def cols(h):
        return slice(h * HD, (h + 1) * HD)

    for h in range(HPD):
        fetch(q_hbm.at[:, cols(h)], qbuf.at[h, a])
    fetch(v_hbm, v_ref)
    fetch(wout_hbm, wout_ref)
    for h in range(HPD):
        fetch(k_hbm.at[:, cols(h)], kvbuf.at[h, zh, x, :TOK])
    early = len(loads)
    for src, dst in (
        (span_hbm, span_ref), (valid_hbm, valid_ref), (step_hbm, step_ref), (span_row_hbm, span_row_ref),
        (order_hbm, order_ref), (lat_hbm, lat_ref), (conv_hbm, conv_ref),
    ):
        fetch(src, dst)
    for copy in loads[:HPD]:
        copy.wait()

    pl.semaphore_wait(barrier, len(greeted))

    def q_copy(h, side, distance, hop):
        block = qbuf.at[h, mod(a - side * way * (distance - hop), NY)]
        n = (0 if side == 1 else 4) + distance - 1
        return remote(block, block, q_send.at[h, n], q_recv.at[h, n], to_y[side * hop])

    def q_wait(h, side, distance):
        q_copy(h, side, distance, min(distance, 2)).wait_recv()

    def z_copy(h):
        block = kvbuf.at[h, zh, x]
        return remote(block, block, z_send.at[h], z_recv.at[h], to_z)

    def x_copy(h, other, step):
        block = kvbuf.at[h, 1 - zh, x] if other else kvbuf.at[:, zh, x]
        n = 3 * other + (1, -1, 2).index(step)
        return remote(block, block, x_send.at[h, n], x_recv.at[h, n], to_x[step])

    started = []

    def start(copy):
        copy.start()
        started.append(copy)

    def q_pass(h):
        q_wait(h, 1, 2)
        start(q_copy(h, 1, 4, 2))
        start(q_copy(h, 1, 3, 1))
        q_wait(h, -1, 2)
        start(q_copy(h, -1, 3, 1))

    def z_pass(h):
        z_copy(h).wait_recv()
        for step in (2, 1, -1):
            start(x_copy(h, 1, step))

    for h in range(HPD):
        for side in (1, -1):
            start(q_copy(h, side, 2, 2))
    for copy in loads[HPD : HPD + 2]:
        copy.wait()
    for h in range(HPD):
        vw = dot(v_ref[:, cols(h)], wout_ref[:, cols(h)], ROWS_BY_KEYS)
        kvbuf[h, zh, x, TOK:] = jnp.concatenate([vw[:PAIRS], vw[PAIRS:]], axis=1).astype(jnp.bfloat16)
    for copy in loads[HPD + 2 : early]:
        copy.wait()
    for h in range(HPD):
        start(z_copy(h))
    for step in (2, 1, -1):
        start(x_copy(0, 0, step))
    for h in range(HPD):
        for side in (1, -1):
            start(q_copy(h, side, 1, 1))

    for copy in loads[early:]:
        copy.wait()
    rels = (0, -1, 1, -2, 2, -3, 3, -4)
    slots = [mod(a + rel * way, NY) for rel in rels]
    lane = lax.broadcasted_iota(jnp.int32, (TOK, TOK), 1)
    row = lax.broadcasted_iota(jnp.int32, (TOK, TOK), 0)
    tile_lane, tile_row = lane[:NY], row[:NY]

    def by_row(scalars):
        tile = jnp.full((NY, TOK), scalars[0])
        for i in range(1, NY):
            tile = jnp.where(tile_row == i, scalars[i], tile)
        return tile

    query_spans = by_row([span_ref[slot_of(b, slot)] for slot in slots])
    for half in range(NZ):
        for j in range(NX):
            key_span = span_ref[slot_of(j * NZ + (zh if half == 0 else 1 - zh), a)]
            live = jnp.where(key_span <= query_spans, valid_ref[key_span], 0)
            bias[half, :, j * TOK : (j + 1) * TOK] = jnp.where(tile_lane < live, 0.0, EXCLUDED)

    vwbuf[:, :, :, TOK:] = jnp.ones((HPD, NZ, HALF, TOK), jnp.bfloat16)
    my_spans = [span_ref[slot_of(b, i)] for i in range(NY)]
    live = by_row([valid_ref[span] for span in my_spans])
    step_rows = jnp.where(tile_lane < live, by_row([step_ref[span] for span in my_spans]), 0.0)
    order = jnp.broadcast_to(order_ref[...].astype(jnp.float32), (TOK, TOK))
    pick = (jnp.transpose(order) == lane.astype(jnp.float32)).astype(jnp.bfloat16)
    halves = (lane == 2 * lax.rem(row, PAIRS) + lax.div(row, PAIRS)).astype(jnp.bfloat16)
    pick = dot(halves, pick)
    lat = dot(pick.astype(jnp.bfloat16), lat_ref[...], ROWS_BY_KEYS)
    lat = jnp.where(g == 0, jnp.concatenate([lat[:PAIRS], lat[PAIRS:]], axis=1), 0.0)

    for h in range(HPD):
        q_pass(h)
    for h in range(HPD):
        z_pass(h)

    def load_vw(h, half):
        for j in range(NX):
            packed = kvbuf[h, zh if half == 0 else 1 - zh, j, TOK:]
            for part in range(2):
                rows = slice(j * TOK + part * PAIRS, j * TOK + (part + 1) * PAIRS)
                vw = packed[:, part * LAT : (part + 1) * LAT]
                vwbuf[h, half, rows, :TOK] = jnp.concatenate([vw, vw], axis=1)

    def scores_of(h, half, places, queries):
        keys = kvbuf[h, zh if half == 0 else 1 - zh, :, :TOK].reshape(HALF, HD)
        scores = dot(queries, keys, ROWS_BY_KEYS)
        return jnp.concatenate(
            [scores[i * TOK : (i + 1) * TOK] + bias[half, n : n + 1] for i, n in enumerate(places)], axis=0
        )

    def weigh(h, half, scores, top):
        return dot(jnp.exp2((scores - top) * SCALE).astype(jnp.bfloat16), vwbuf[h, half])

    def stacked(ref, h, places):
        return jnp.concatenate([ref[h, slots[n]] for n in places], axis=0)

    def row_max(scores):
        return jnp.max(scores, axis=1, keepdims=True)

    def attend_own(h, places):
        scores = scores_of(h, 0, places, stacked(qbuf, h, places))
        top = row_max(scores)
        out = weigh(h, 0, scores, top)
        for i, n in enumerate(places):
            acc[h, slots[n]] = out[i * TOK : (i + 1) * TOK]
            tops[h, slots[n]] = top[i * TOK : (i + 1) * TOK]

    def finish(h, places, top, out):
        total = out[:, TOK:]
        lse = top * SCALE + jnp.log2(total)
        out = (out[:, :TOK] / total).astype(jnp.bfloat16)
        for i, n in enumerate(places):
            obuf[h, slots[n]] = out[i * TOK : (i + 1) * TOK]
        return [lse[i * TOK : (i + 1) * TOK] for i in range(len(places))]

    def attend_others(h, places):
        scores = scores_of(h, 1, places, stacked(qbuf, h, places))
        before = stacked(tops, h, places)
        top = jnp.maximum(row_max(scores), before)
        out = weigh(h, 1, scores, top) + jnp.exp2((before - top) * SCALE) * stacked(acc, h, places)
        return finish(h, places, top, out)

    def attend_all(h, places):
        queries = stacked(qbuf, h, places)
        scores = [scores_of(h, half, places, queries) for half in range(NZ)]
        top = jnp.maximum(row_max(scores[0]), row_max(scores[1]))
        return finish(h, places, top, sum(weigh(h, half, scores[half], top) for half in range(NZ)))

    def lse_copy(h, rel):
        block = lsebuf.at[h, a]
        return remote(block, block, s_send.at[h], s_recv.at[h], (slot_of(b, mod(a + rel, NY)), g))

    def lse_all(h):
        block = lsebuf.at[h, : NY - 1]
        return remote(block, block, s_send.at[h], s_recv.at[h], to_y[1])

    def lse_send(h, columns, places):
        stats = jnp.zeros((TOK, TOK), jnp.float32)
        for column, index in zip(columns, [slots[n] for n in places]):
            stats = jnp.where(lane == index, column, stats)
        lsebuf[h, a] = jnp.transpose(stats)[:NY]
        for rel in (4, 3, 5, 2, 6, 1, 7):
            lse_copy(h, rel).start()

    for step in (1, -1, 2):
        x_copy(0, 0, step).wait_recv()
    for h in range(HPD):
        load_vw(h, 0)
        q_wait(h, 1, 1)
        q_wait(h, -1, 1)
        attend_own(h, (0, 1))
        attend_own(h, (2, 3, 4))
    for h in range(HPD):
        q_wait(h, 1, 3)
        q_wait(h, -1, 3)
        q_wait(h, 1, 4)
    for h in range(HPD):
        attend_own(h, (5, 6, 7))
    for h in range(HPD):
        for step in (1, -1, 2):
            x_copy(h, 1, step).wait_recv()
        load_vw(h, 1)
        columns = sum((attend_others(h, (2 * n, 2 * n + 1)) for n in range(NY // 2)), [])
        lse_send(h, columns, range(NY))

    for device in head_peers:
        pl.semaphore_signal(ready, inc=1, device_id=device, device_id_type=MESH)

    for h in range(HPD):
        lse_all(h).wait_recv()
    shares = []
    for h in range(HPD):
        parts = lsebuf[h]
        top = jnp.max(parts, axis=0)
        total = jnp.sum(jnp.exp2(parts - top[None]), axis=0)
        shares.append(jnp.exp2(lsebuf[h, a] - top) / total * step_rows)
    for i in range(NY):
        left = jnp.concatenate([(pick * share[i : i + 1]).astype(jnp.bfloat16) for share in shares], axis=1)
        term = dot(left, jnp.concatenate([obuf[h, i] for h in range(HPD)], axis=0))
        term = jnp.where(lane[:PAIRS] < LAT, term[:PAIRS], term[PAIRS:]) + jnp.where(a == i, lat, 0.0)
        for gg in range(NG):
            stage[gg // 2, pl.ds(gg % 2 * NY + i, NY, stride=2 * NY)] = term[gg * NY : (gg + 1) * NY]
    sendbuf[...] = stage[...].astype(jnp.bfloat16)

    pl.semaphore_wait(ready, len(head_peers))

    def owner(aa):
        return pl.ds(pl.multiple_of(aa * 2 * NY, 2 * NY), 2 * NY)

    def c_copy(rel):
        aa, gg = partner(rel)
        return remote(sendbuf.at[lax.div(gg, 2), owner(aa)], c1buf.at[rel - 1], c_send, c_recv, (slot_of(b, aa), gg))

    def hops(rel):
        return min(rel // NL, NY - rel // NL) + min(rel % NL, NL - rel % NL)

    for rel in sorted(range(1, NY * NL), key=hops, reverse=True):
        c_copy(rel).start()
    sums = remote(c1buf, c1buf, c_send, c_recv, to_core)
    sums.wait_recv()
    total = stage[zl, owner(a)] + jnp.sum(c1buf[...].astype(jnp.float32), axis=0)
    sumbuf[...] = total.reshape(2, NY, TOK)
    pair_copy = remote(sumbuf.at[1 - core], pairbuf, p_send, p_recv, to_core)
    pair_copy.start()
    pair_copy.wait_recv()
    ubuf[...] = sumbuf[core] + pairbuf[...]

    def d_copy(gg):
        return remote(ubuf, dbuf.at[b], d_send.at[gg], d_recv.at[b], (slot_of(g, a), gg))

    def own_target(gg):
        return jnp.logical_and(self_last, gg == g)

    for gg in range(NG):
        @pl.when(jnp.logical_not(own_target(gg)))
        def _():
            d_copy(gg).start()

    @pl.when(self_last)
    def _():
        dbuf[b] = ubuf[...]

    zeros = jnp.zeros((LAT, LAT), jnp.bfloat16)
    taps = []
    for k in range(KT):
        tap = conv_ref[k]
        taps.append(jnp.concatenate([tap, zeros], axis=1))
        taps.append(jnp.concatenate([zeros, tap], axis=1))
    taps = jnp.concatenate(taps, axis=0)
    time = lax.broadcasted_iota(jnp.int32, (NSLOT, NSLOT), 0)
    spans = jnp.broadcast_to(span_row_ref[...], (NSLOT, NSLOT))
    orders = [(spans == time - k).astype(jnp.bfloat16) for k in range(KT)]

    for copy in started:
        copy.wait_send()
    for h in range(HPD):
        lse_all(h).wait_send()
    pair_copy.wait_send()
    sums.wait_send()

    for bb in range(NB):
        @pl.when(jnp.logical_not(jnp.logical_and(self_last, bb == b)))
        def _():
            remote(ubuf, dbuf.at[bb], d_send.at[0], d_recv.at[bb], to_z).wait_recv()
    updated = dbuf[...].reshape(NSLOT, 2 * LAT).astype(jnp.bfloat16)
    shifted = [dot(order, updated).astype(jnp.bfloat16) for order in orders]
    features = dot(jnp.concatenate(shifted, axis=1), taps).astype(jnp.bfloat16)
    denoised = shifted[0]
    for p in range(2):
        part = slice(p * LAT, (p + 1) * LAT)
        out_ref[p] = jnp.concatenate([denoised[:, part], features[:, part]], axis=1)

    for gg in range(NG):
        @pl.when(jnp.logical_not(own_target(gg)))
        def _():
            d_copy(gg).wait_send()


def local(
    queries, keys, values, latents, out_weight, step_size, conv_weight, span_of_slot, valid_count, decoder_order
):
    vmem, anywhere = pl.BlockSpec(memory_space=pltpu.VMEM), pl.BlockSpec(memory_space=pl.ANY)
    dma = pltpu.SemaphoreType.DMA
    bf16, f32, i32 = jnp.bfloat16, jnp.float32, jnp.int32
    both = pl.pallas_call(
        kernel,
        out_shape=jax.ShapeDtypeStruct((2, NSLOT, 2 * LAT), bf16),
        in_specs=[anywhere] * 11,
        out_specs=vmem,
        scratch_shapes=[
            pltpu.VMEM((TOK, HPD * HD), bf16),
            pltpu.VMEM((LAT, TOK), bf16),
            pltpu.VMEM((LAT, HPD * HD), bf16),
            pltpu.VMEM((KT, LAT, LAT), bf16),
            pltpu.VMEM((1, NSLOT), i32),
            pltpu.VMEM((1, TOK), i32),
            pltpu.SMEM((NSLOT,), i32),
            pltpu.SMEM((NSLOT,), i32),
            pltpu.SMEM((NSLOT,), f32),
            pltpu.VMEM((HPD, NY, TOK, HD), bf16),
            pltpu.VMEM((HPD, NZ, NX, TOK + PAIRS, HD), bf16),
            pltpu.VMEM((HPD, NZ, HALF, 2 * TOK), bf16),
            pltpu.VMEM((HPD, NY, TOK, 2 * TOK), f32),
            pltpu.VMEM((HPD, NY, TOK, 1), f32),
            pltpu.VMEM((HPD, NY, TOK, TOK), bf16),
            pltpu.VMEM((NZ, NY, HALF), f32),
            pltpu.VMEM((HPD, NY, NY, TOK), f32),
            pltpu.VMEM((NL, 2 * NY * NY, TOK), f32),
            pltpu.VMEM((NL, 2 * NY * NY, TOK), bf16),
            pltpu.VMEM((NY * NL - 1, 2 * NY, TOK), bf16),
            pltpu.VMEM((2, NY, TOK), f32),
            pltpu.VMEM((NY, TOK), f32),
            pltpu.VMEM((NY, TOK), f32),
            pltpu.VMEM((NB, NY, TOK), f32),
            pltpu.SemaphoreType.REGULAR,
            dma((15,)),
            dma((HPD, 7)), dma((HPD, 7)),
            dma((HPD,)), dma((HPD,)),
            dma((HPD, 6)), dma((HPD, 6)),
            dma((HPD,)), dma((HPD,)),
            dma, dma,
            dma, dma,
            dma((NG,)), dma((NB,)),
        ],
        compiler_params=pltpu.CompilerParams(
            collective_id=0, has_side_effects=True, vmem_limit_bytes=54 * 2**20
        ),
        name="span_attention",
    )(
        queries, keys, values, latents.T, out_weight.T, conv_weight,
        span_of_slot.reshape(1, NSLOT), decoder_order.reshape(1, TOK),
        span_of_slot, valid_count, step_size,
    )
    return both[:, :, :LAT], both[:, :, LAT:]


def solution(mesh):
    return jax.shard_map(
        local,
        mesh=mesh,
        in_specs=(
            P("tm", "head"),
            P("tm", "head"),
            P("tm", "head"),
            P("tm", None),
            P("head", None),
            P(),
            P(None, None, "head"),
            P(),
            P(),
            P(),
        ),
        out_specs=(P("tm", None, None), P("tm", None, "head")),
        check_vma=False,
    )
```

```python
import jax
import jax.numpy as jnp
from jax import lax
from jax.experimental import pallas as pl
from jax.experimental.pallas import tpu as pltpu
from jax.sharding import PartitionSpec as P

HD = 128
HPD = 3
TOK = 128
LAT = 64
KT = 3
NX, NZ, NY = 4, 2, 8
NB = NX * NZ
NG = 8
NL = NG // 2
PAIRS = TOK // 2
NSLOT = NB * NY
HALF = NX * TOK
EXCLUDED = -1e30
SCALE = 1.4426950408889634 / HD**0.5
MESH = pl.DeviceIdType.MESH
ROWS_BY_KEYS = (((1,), (1,)), ((), ()))


def mod(value, size):
    return lax.rem(value + 2 * size, size)


def remote(src, dst, send, recv, device):
    return pltpu.make_async_remote_copy(
        src_ref=src, dst_ref=dst, send_sem=send, recv_sem=recv, device_id=device, device_id_type=MESH
    )


def dot(left, right, dims=(((1,), (0,)), ((), ()))):
    return lax.dot_general(left, right, dims, preferred_element_type=jnp.float32)


def kernel(
    q_hbm, k_hbm, v_hbm, lat_hbm, wout_hbm, conv_hbm, span_row_hbm, order_hbm, span_hbm, valid_hbm, step_hbm,
    out_ref,
    v_ref, lat_ref, wout_ref, conv_ref, span_row_ref, order_ref, span_ref, valid_ref, step_ref,
    qbuf, kvbuf, vwbuf, acc, tops, obuf, bias, lsebuf, stage, sendbuf, c1buf, sumbuf, pairbuf, ubuf, dbuf,
    ready, load, q_send, q_recv, z_send, z_recv, x_send, x_recv, s_send, s_recv,
    p_send, p_recv, c_send, c_recv, d_send, d_recv,
):
    tm = lax.axis_index("tm")
    g = lax.axis_index("head")
    b, a = lax.div(tm, NY), lax.rem(tm, NY)
    x, zh = lax.div(b, NZ), lax.rem(b, NZ)
    zl, core = lax.div(g, 2), lax.rem(g, 2)
    way = 1 - 2 * core

    def slot_of(bb, aa):
        return bb * NY + aa

    to_y = {s: (slot_of(b, mod(a + s * way, NY)), g) for s in (1, -1, 2, -2)}
    to_x = {s: (slot_of(mod(x + s, NX) * NZ + zh, a), g) for s in (1, -1, 2)}
    to_z = (slot_of(x * NZ + 1 - zh, a), g)
    to_core = (tm, g + way)
    self_last = b == g

    barrier = pltpu.get_barrier_semaphore()
    head_peers = [(tm, mod(g + rel, NG)) for rel in range(1, NG)]
    greeted = [to_z, to_x[1], to_x[-1], to_x[2], *to_y.values(), *head_peers]
    for device in greeted:
        pl.semaphore_signal(barrier, inc=1, device_id=device, device_id_type=MESH)

    def partner(rel):
        return mod(a + rel // NL, NY), mod(zl + rel % NL, NL) * 2 + core

    loads = []

    def fetch(src, dst):
        copy = pltpu.make_async_copy(src, dst, load.at[len(loads)])
        copy.start()
        loads.append(copy)

    def cols(h):
        return slice(h * HD, (h + 1) * HD)

    for h in range(HPD):
        fetch(q_hbm.at[:, cols(h)], qbuf.at[h, a])
    fetch(v_hbm, v_ref)
    fetch(wout_hbm, wout_ref)
    for h in range(HPD):
        fetch(k_hbm.at[:, cols(h)], kvbuf.at[h, zh, x, :TOK])
    early = len(loads)
    for src, dst in (
        (span_hbm, span_ref), (valid_hbm, valid_ref), (step_hbm, step_ref), (span_row_hbm, span_row_ref),
        (order_hbm, order_ref), (lat_hbm, lat_ref), (conv_hbm, conv_ref),
    ):
        fetch(src, dst)
    for copy in loads[:HPD]:
        copy.wait()

    pl.semaphore_wait(barrier, len(greeted))

    def q_copy(h, side, distance, hop):
        block = qbuf.at[h, mod(a - side * way * (distance - hop), NY)]
        n = (0 if side == 1 else 4) + distance - 1
        return remote(block, block, q_send.at[h, n], q_recv.at[h, n], to_y[side * hop])

    def q_wait(h, side, distance):
        q_copy(h, side, distance, min(distance, 2)).wait_recv()

    def z_copy(h):
        block = kvbuf.at[h, zh, x]
        return remote(block, block, z_send.at[h], z_recv.at[h], to_z)

    def x_copy(h, other, step):
        block = kvbuf.at[h, 1 - zh, x] if other else kvbuf.at[:, zh, x]
        n = 3 * other + (1, -1, 2).index(step)
        return remote(block, block, x_send.at[h, n], x_recv.at[h, n], to_x[step])

    started = []

    def start(copy):
        copy.start()
        started.append(copy)

    def q_pass(h):
        q_wait(h, 1, 2)
        start(q_copy(h, 1, 4, 2))
        start(q_copy(h, 1, 3, 1))
        q_wait(h, -1, 2)
        start(q_copy(h, -1, 3, 1))

    def z_pass(h):
        z_copy(h).wait_recv()
        for step in (2, 1, -1):
            start(x_copy(h, 1, step))

    for h in range(HPD):
        for side in (1, -1):
            start(q_copy(h, side, 2, 2))
    for copy in loads[HPD : HPD + 2]:
        copy.wait()
    for h in range(HPD):
        vw = dot(v_ref[:, cols(h)], wout_ref[:, cols(h)], ROWS_BY_KEYS)
        kvbuf[h, zh, x, TOK:] = jnp.concatenate([vw[:PAIRS], vw[PAIRS:]], axis=1).astype(jnp.bfloat16)
    for copy in loads[HPD + 2 : early]:
        copy.wait()
    for h in range(HPD):
        start(z_copy(h))
    for step in (2, 1, -1):
        start(x_copy(0, 0, step))
    for h in range(HPD):
        for side in (1, -1):
            start(q_copy(h, side, 1, 1))

    for copy in loads[early:]:
        copy.wait()
    rels = (0, -1, 1, -2, 2, -3, 3, -4)
    slots = [mod(a + rel * way, NY) for rel in rels]
    lane = lax.broadcasted_iota(jnp.int32, (TOK, TOK), 1)
    row = lax.broadcasted_iota(jnp.int32, (TOK, TOK), 0)
    tile_lane, tile_row = lane[:NY], row[:NY]

    def by_row(scalars):
        tile = jnp.full((NY, TOK), scalars[0])
        for i in range(1, NY):
            tile = jnp.where(tile_row == i, scalars[i], tile)
        return tile

    query_spans = by_row([span_ref[slot_of(b, slot)] for slot in slots])
    for half in range(NZ):
        for j in range(NX):
            key_span = span_ref[slot_of(j * NZ + (zh if half == 0 else 1 - zh), a)]
            live = jnp.where(key_span <= query_spans, valid_ref[key_span], 0)
            bias[half, :, j * TOK : (j + 1) * TOK] = jnp.where(tile_lane < live, 0.0, EXCLUDED)

    vwbuf[:, :, :, TOK:] = jnp.ones((HPD, NZ, HALF, TOK), jnp.bfloat16)
    my_spans = [span_ref[slot_of(b, i)] for i in range(NY)]
    live = by_row([valid_ref[span] for span in my_spans])
    step_rows = jnp.where(tile_lane < live, by_row([step_ref[span] for span in my_spans]), 0.0)
    order = jnp.broadcast_to(order_ref[...].astype(jnp.float32), (TOK, TOK))
    pick = (jnp.transpose(order) == lane.astype(jnp.float32)).astype(jnp.bfloat16)
    halves = (lane == 2 * lax.rem(row, PAIRS) + lax.div(row, PAIRS)).astype(jnp.bfloat16)
    pick = dot(halves, pick).astype(jnp.bfloat16)
    lat = dot(pick, lat_ref[...], ROWS_BY_KEYS)
    lat = jnp.where(g == 0, jnp.concatenate([lat[:PAIRS], lat[PAIRS:]], axis=1), 0.0)

    for h in range(HPD):
        q_pass(h)
    for h in range(HPD):
        z_pass(h)

    def load_vw(h, half):
        for j in range(NX):
            packed = kvbuf[h, zh if half == 0 else 1 - zh, j, TOK:]
            for part in range(2):
                rows = slice(j * TOK + part * PAIRS, j * TOK + (part + 1) * PAIRS)
                vw = packed[:, part * LAT : (part + 1) * LAT]
                vwbuf[h, half, rows, :TOK] = jnp.concatenate([vw, vw], axis=1)

    def scores_of(h, half, places, queries):
        keys = kvbuf[h, zh if half == 0 else 1 - zh, :, :TOK].reshape(HALF, HD)
        scores = dot(queries, keys, ROWS_BY_KEYS)
        return jnp.concatenate(
            [scores[i * TOK : (i + 1) * TOK] + bias[half, n : n + 1] for i, n in enumerate(places)], axis=0
        )

    def weigh(h, half, scores, top):
        return dot(jnp.exp2((scores - top) * SCALE).astype(jnp.bfloat16), vwbuf[h, half])

    def stacked(ref, h, places):
        return jnp.concatenate([ref[h, slots[n]] for n in places], axis=0)

    def row_max(scores):
        return jnp.max(scores, axis=1, keepdims=True)

    def attend_own(h, places):
        scores = scores_of(h, 0, places, stacked(qbuf, h, places))
        top = row_max(scores)
        out = weigh(h, 0, scores, top)
        for i, n in enumerate(places):
            acc[h, slots[n]] = out[i * TOK : (i + 1) * TOK]
            tops[h, slots[n]] = top[i * TOK : (i + 1) * TOK]

    def finish(h, places, top, out):
        total = out[:, TOK:]
        lse = top * SCALE + jnp.log2(total)
        out = (out[:, :TOK] / total).astype(jnp.bfloat16)
        for i, n in enumerate(places):
            obuf[h, slots[n]] = out[i * TOK : (i + 1) * TOK]
        return [lse[i * TOK : (i + 1) * TOK] for i in range(len(places))]

    def attend_others(h, places):
        scores = scores_of(h, 1, places, stacked(qbuf, h, places))
        before = stacked(tops, h, places)
        top = jnp.maximum(row_max(scores), before)
        out = weigh(h, 1, scores, top) + jnp.exp2((before - top) * SCALE) * stacked(acc, h, places)
        return finish(h, places, top, out)

    def attend_all(h, places):
        queries = stacked(qbuf, h, places)
        scores = [scores_of(h, half, places, queries) for half in range(NZ)]
        top = jnp.maximum(row_max(scores[0]), row_max(scores[1]))
        return finish(h, places, top, sum(weigh(h, half, scores[half], top) for half in range(NZ)))

    def lse_copy(h, rel):
        block = lsebuf.at[h, a]
        return remote(block, block, s_send.at[h], s_recv.at[h], (slot_of(b, mod(a + rel, NY)), g))

    def lse_all(h):
        block = lsebuf.at[h, : NY - 1]
        return remote(block, block, s_send.at[h], s_recv.at[h], to_y[1])

    def lse_send(h, columns, places):
        stats = jnp.zeros((TOK, TOK), jnp.float32)
        for column, index in zip(columns, [slots[n] for n in places]):
            stats = jnp.where(lane == index, column, stats)
        lsebuf[h, a] = jnp.transpose(stats)[:NY]
        for rel in (4, 3, 5, 2, 6, 1, 7):
            lse_copy(h, rel).start()

    for step in (1, -1, 2):
        x_copy(0, 0, step).wait_recv()
    for h in range(HPD):
        load_vw(h, 0)
        q_wait(h, 1, 1)
        q_wait(h, -1, 1)
        attend_own(h, (0, 1))
        attend_own(h, (2, 3, 4))
    for h in range(HPD):
        q_wait(h, 1, 3)
        q_wait(h, -1, 3)
        q_wait(h, 1, 4)
    for h in range(HPD):
        attend_own(h, (5, 6, 7))
    for h in range(HPD):
        for step in (1, -1, 2):
            x_copy(h, 1, step).wait_recv()
        load_vw(h, 1)
        columns = sum((attend_others(h, (2 * n, 2 * n + 1)) for n in range(NY // 2)), [])
        lse_send(h, columns, range(NY))

    for device in head_peers:
        pl.semaphore_signal(ready, inc=1, device_id=device, device_id_type=MESH)

    for h in range(HPD):
        lse_all(h).wait_recv()
    shares = []
    for h in range(HPD):
        parts = lsebuf[h]
        top = jnp.max(parts, axis=0)
        total = jnp.sum(jnp.exp2(parts - top[None]), axis=0)
        shares.append(jnp.exp2(lsebuf[h, a] - top) / total * step_rows)
    for i in range(NY):
        left = jnp.concatenate([pick * share[i : i + 1].astype(jnp.bfloat16) for share in shares], axis=1)
        term = dot(left, jnp.concatenate([obuf[h, i] for h in range(HPD)], axis=0))
        term = jnp.where(lane[:PAIRS] < LAT, term[:PAIRS], term[PAIRS:]) + jnp.where(a == i, lat, 0.0)
        for gg in range(NG):
            stage[gg // 2, pl.ds(gg % 2 * NY + i, NY, stride=2 * NY)] = term[gg * NY : (gg + 1) * NY]
    sendbuf[...] = stage[...].astype(jnp.bfloat16)

    pl.semaphore_wait(ready, len(head_peers))

    def owner(aa):
        return pl.ds(pl.multiple_of(aa * 2 * NY, 2 * NY), 2 * NY)

    def c_copy(rel):
        aa, gg = partner(rel)
        return remote(sendbuf.at[lax.div(gg, 2), owner(aa)], c1buf.at[rel - 1], c_send, c_recv, (slot_of(b, aa), gg))

    def hops(rel):
        return min(rel // NL, NY - rel // NL) + min(rel % NL, NL - rel % NL)

    for rel in sorted(range(1, NY * NL), key=hops, reverse=True):
        c_copy(rel).start()
    sums = remote(c1buf, c1buf, c_send, c_recv, to_core)
    sums.wait_recv()
    total = stage[zl, owner(a)] + jnp.sum(c1buf[...].astype(jnp.float32), axis=0)
    sumbuf[...] = total.reshape(2, NY, TOK)
    pair_copy = remote(sumbuf.at[1 - core], pairbuf, p_send, p_recv, to_core)
    pair_copy.start()
    pair_copy.wait_recv()
    ubuf[...] = sumbuf[core] + pairbuf[...]

    def d_copy(gg):
        return remote(ubuf, dbuf.at[b], d_send.at[gg], d_recv.at[b], (slot_of(g, a), gg))

    def own_target(gg):
        return jnp.logical_and(self_last, gg == g)

    for gg in range(NG):
        @pl.when(jnp.logical_not(own_target(gg)))
        def _():
            d_copy(gg).start()

    @pl.when(self_last)
    def _():
        dbuf[b] = ubuf[...]

    zeros = jnp.zeros((LAT, LAT), jnp.bfloat16)
    taps = []
    for k in range(KT):
        tap = conv_ref[k]
        taps.append(jnp.concatenate([tap, zeros], axis=1))
        taps.append(jnp.concatenate([zeros, tap], axis=1))
    taps = jnp.concatenate(taps, axis=0)
    time = lax.broadcasted_iota(jnp.int32, (NSLOT, NSLOT), 0)
    spans = jnp.broadcast_to(span_row_ref[...], (NSLOT, NSLOT))
    orders = [(spans == time - k).astype(jnp.bfloat16) for k in range(KT)]

    for copy in started:
        copy.wait_send()
    for h in range(HPD):
        lse_all(h).wait_send()
    pair_copy.wait_send()
    sums.wait_send()

    for bb in range(NB):
        @pl.when(jnp.logical_not(jnp.logical_and(self_last, bb == b)))
        def _():
            remote(ubuf, dbuf.at[bb], d_send.at[0], d_recv.at[bb], to_z).wait_recv()
    updated = dbuf[...].reshape(NSLOT, 2 * LAT).astype(jnp.bfloat16)
    shifted = [dot(order, updated).astype(jnp.bfloat16) for order in orders]
    features = dot(jnp.concatenate(shifted, axis=1), taps).astype(jnp.bfloat16)
    denoised = shifted[0]
    for p in range(2):
        part = slice(p * LAT, (p + 1) * LAT)
        out_ref[p] = jnp.concatenate([denoised[:, part], features[:, part]], axis=1)

    for gg in range(NG):
        @pl.when(jnp.logical_not(own_target(gg)))
        def _():
            d_copy(gg).wait_send()


def local(
    queries, keys, values, latents, out_weight, step_size, conv_weight, span_of_slot, valid_count, decoder_order
):
    vmem, anywhere = pl.BlockSpec(memory_space=pltpu.VMEM), pl.BlockSpec(memory_space=pl.ANY)
    dma = pltpu.SemaphoreType.DMA
    bf16, f32, i32 = jnp.bfloat16, jnp.float32, jnp.int32
    both = pl.pallas_call(
        kernel,
        out_shape=jax.ShapeDtypeStruct((2, NSLOT, 2 * LAT), bf16),
        in_specs=[anywhere] * 11,
        out_specs=vmem,
        scratch_shapes=[
            pltpu.VMEM((TOK, HPD * HD), bf16),
            pltpu.VMEM((LAT, TOK), bf16),
            pltpu.VMEM((LAT, HPD * HD), bf16),
            pltpu.VMEM((KT, LAT, LAT), bf16),
            pltpu.VMEM((1, NSLOT), i32),
            pltpu.VMEM((1, TOK), i32),
            pltpu.SMEM((NSLOT,), i32),
            pltpu.SMEM((NSLOT,), i32),
            pltpu.SMEM((NSLOT,), f32),
            pltpu.VMEM((HPD, NY, TOK, HD), bf16),
            pltpu.VMEM((HPD, NZ, NX, TOK + PAIRS, HD), bf16),
            pltpu.VMEM((HPD, NZ, HALF, 2 * TOK), bf16),
            pltpu.VMEM((HPD, NY, TOK, 2 * TOK), f32),
            pltpu.VMEM((HPD, NY, TOK, 1), f32),
            pltpu.VMEM((HPD, NY, TOK, TOK), bf16),
            pltpu.VMEM((NZ, NY, HALF), f32),
            pltpu.VMEM((HPD, NY, NY, TOK), f32),
            pltpu.VMEM((NL, 2 * NY * NY, TOK), f32),
            pltpu.VMEM((NL, 2 * NY * NY, TOK), bf16),
            pltpu.VMEM((NY * NL - 1, 2 * NY, TOK), bf16),
            pltpu.VMEM((2, NY, TOK), f32),
            pltpu.VMEM((NY, TOK), f32),
            pltpu.VMEM((NY, TOK), f32),
            pltpu.VMEM((NB, NY, TOK), f32),
            pltpu.SemaphoreType.REGULAR,
            dma((15,)),
            dma((HPD, 7)), dma((HPD, 7)),
            dma((HPD,)), dma((HPD,)),
            dma((HPD, 6)), dma((HPD, 6)),
            dma((HPD,)), dma((HPD,)),
            dma, dma,
            dma, dma,
            dma((NG,)), dma((NB,)),
        ],
        compiler_params=pltpu.CompilerParams(
            collective_id=0, has_side_effects=True, vmem_limit_bytes=54 * 2**20
        ),
        name="span_attention",
    )(
        queries, keys, values, latents.T, out_weight.T, conv_weight,
        span_of_slot.reshape(1, NSLOT), decoder_order.reshape(1, TOK),
        span_of_slot, valid_count, step_size,
    )
    return both[:, :, :LAT], both[:, :, LAT:]


def solution(mesh):
    return jax.shard_map(
        local,
        mesh=mesh,
        in_specs=(
            P("tm", "head"),
            P("tm", "head"),
            P("tm", "head"),
            P("tm", None),
            P("head", None),
            P(),
            P(None, None, "head"),
            P(),
            P(),
            P(),
        ),
        out_specs=(P("tm", None, None), P("tm", None, "head")),
        check_vma=False,
    )
```
